512 devices in a mesh: dp: 16 (over y, core), seq: 32 (over x, z).
Axes of the slice: x: 4, y: 8, z: 8, core: 2. Of those that a mesh axis runs over, the one named last changes fastest.
Arguments:
- frame_in: bfloat16 [16, 4608, 1024], P('dp', 'seq'), may hold values from -120 to 120
- token_ids: int32 [16, 32, 60], P('dp', 'seq'), may hold values from 0 to 3327
- durations: int32 [16, 32, 60], P('dp', 'seq'), may hold values from 1 to 4, 144 in all within a row
- valid_len: int32 [16], P('dp'), may hold values from 1152 to 4608, as said below
- t_bin: int32 [16], P('dp'), may hold values from 0 to 63
- token_table: bfloat16 [3328, 512], P('seq'), may hold values from -6 to 6
- enc_weight: bfloat16 [512, 1024], replicated, may hold values from -0.25 to 0.25
- mod_table: float32 [64, 2048], replicated, may hold values from -1.2 to 2.5
- w_query: bfloat16 [1024, 512], P('seq'), may hold values from -0.1875 to 0.1875
- w_key: bfloat16 [1024, 512], P('seq'), may hold values from -0.1875 to 0.1875
- w_value: bfloat16 [1024, 512], P('seq'), may hold values from -0.1875 to 0.1875
- attn_grad: bfloat16 [16, 4608, 512], P('dp', 'seq'), may hold values from -6 to 6
Outputs:
- attn_out: bfloat16 [16, 4608, 512], P('dp', 'seq')
- frame_grad: bfloat16 [16, 4608, 1024], P('dp', 'seq')
- query_weight_grad: float32 [1024, 512], P('seq')
- key_weight_grad: float32 [1024, 512], P('seq')
- value_weight_grad: float32 [1024, 512], P('seq')
The draws below stay inside these ranges and needn't reach their ends.
Inputs may be any that keep to these rules, and one draw needn't show every extreme that they name: In every slab the 60 durations sum to 144, so each token's frames lie in its own slab; some token lasts 4 frames. `valid_len`: some recording is valid over all 4608 frames.
All inputs are finite; a program needn't handle non-finite values.
Results may differ from the reference program's by a relative error of at most 0.017.
The reference program's roundings to bfloat16 on the way count: a program that leaves them out, or rounds other values in their place, can miss the bound.
Values may be sent and summed in bfloat16 or wider, within the bound.
A program may use at most 64 MiB of HBM per device.

```python
import math
import jax
import jax.numpy as jnp
import numpy as np
from jax import lax

D = 1024
ENC = 512
HEADS = 8
HD = 64
BLK = 48
NBINS = 64
F_DEV = 144
TOK_DEV = 60
RECS = 16
FRAMES = 4608
VOCAB = 3328
QW = 512
N_SEQ = 32


def draw_frame_in(key, part):
    key_base, key_rows, key_cols = jax.random.split(key, 3)
    row_scale = jnp.exp(jax.random.uniform(key_rows, (RECS, FRAMES, 1), jnp.float32, 0.0, math.log(10.0)))
    col_scale = jnp.exp(jax.random.uniform(key_cols, (1, 1, D), jnp.float32, 0.0, math.log(10.0)))
    base_vals = jnp.clip(jax.random.normal(key_base, (RECS, FRAMES, D), jnp.float32), -4.0, 4.0)
    return (0.3 * base_vals * row_scale * col_scale).astype(jnp.bfloat16)


def draw_valid_len(key, part):
    key_len, key_full = jax.random.split(jax.random.fold_in(key, 17), 2)
    lengths = jax.random.randint(key_len, (RECS,), FRAMES // 4, FRAMES + 1)
    full_rec = jax.random.randint(key_full, (), 0, RECS)
    rec_index = jnp.arange(RECS, dtype=jnp.int32)
    return jnp.where(rec_index == full_rec, FRAMES, lengths).astype(jnp.int32)


def draw_mod_table(key, part):
    key_shift, key_gain = jax.random.split(key, 2)
    shift_vals = 0.3 * jnp.clip(jax.random.normal(key_shift, (NBINS, D), jnp.float32), -4.0, 4.0)
    gain_vals = 0.3 * jnp.clip(jax.random.normal(key_gain, (NBINS, D), jnp.float32), -3.0, 3.0)
    return jnp.concatenate([gain_vals, shift_vals], axis=1)


def place_ends(values, rng, smallest, top_value):
    extent = values.shape
    spot = [jax.random.randint(jax.random.fold_in(rng, axis), (), 0, extent[axis]) for axis in range(len(extent))]
    values = values.at[tuple(spot)].set(smallest)
    longest = extent.index(max(extent))
    spot[longest] = (spot[longest] + 1) % extent[longest]
    return values.at[tuple(spot)].set(top_value)


def level_of(key, dims, cuts, least, largest):
    gain, own = 1.0, jax.random.fold_in(key, 6)
    for dim, blocks in cuts:
        draws = jnp.exp(jax.random.uniform(jax.random.fold_in(own, dim), (blocks,), jnp.float32, least / len(cuts), largest / len(cuts)))
        gain = gain * jnp.repeat(draws, dims[dim] // blocks).reshape([-1 if axis == dim else 1 for axis in range(len(dims))])
    return gain


def rank_table(number_of, lean):
    portions = [(1 << 20) // math.isqrt(standing ** lean) + 1 for standing in range(1, number_of + 1)]
    deviation = 1 + sum(portions) // (1 << 30)
    return np.cumsum(np.array([max(1, weight // deviation) for weight in portions]))


def ranked_ids(own_key, dims, amount, skew):
    grid = rank_table(amount, skew)
    ticket = jax.random.randint(jax.random.fold_in(own_key, 1), dims, 0, int(grid[amount - 1]))
    grade = jnp.searchsorted(jnp.asarray(grid, jnp.int32), ticket, side="right")
    return jax.random.permutation(jax.random.fold_in(own_key, 2), amount)[grade].astype(jnp.int32)


def length_profile(number_of, total, bound, lean):
    weights = [(1 << 20) // math.isqrt(grade ** lean) + 1 for grade in range(2, number_of + 1)]
    surplus, counts = total - bound - (number_of - 1), [1] * (number_of - 1)
    while surplus > 0:
        movable = [i for i in range(number_of - 1) if counts[i] < bound]
        mass, remaining = sum([weights[i] for i in movable]), surplus
        for i in movable:
            addition = min(bound - counts[i], max(1, remaining * weights[i] // mass), surplus)
            counts[i] = counts[i] + addition
            surplus = surplus - addition
    return np.array([bound] + counts)


def ragged_sizes(own_key, count, total, most, slope):
    if count == 2:
        one = jax.random.randint(own_key, (), max(1, total - most), min(most, total - 1) + 1)
        return jnp.stack([one, total - one])
    sizes = jnp.asarray(length_profile(count, total, most, slope), jnp.int32)
    couples = (count - 1) // 2
    donor, receiver = sizes[1:1 + 2 * couples:2], sizes[2:2 + 2 * couples:2]
    slack = jnp.minimum(donor - 1, most - receiver)
    shifted = jax.random.randint(jax.random.fold_in(own_key, 1), (couples,), 0, 1 << 20) % (slack + 1)
    sizes = sizes.at[1:1 + 2 * couples:2].set(donor - shifted).at[2:2 + 2 * couples:2].set(receiver + shifted)
    return sizes[jax.random.permutation(jax.random.fold_in(own_key, 2), count)]


def centred(rng, extent, deviation, most, cuts=(), kind=jnp.bfloat16):
    array = jax.random.normal(rng, extent, jnp.float32) * deviation
    if len(cuts) > 0:
        array = level_of(rng, extent, cuts, -0.22, 0.18) * array
    return jnp.clip(array, min=-most, max=most).astype(kind)


def setup_inputs(seed: int = 0) -> dict:
    key_list = jax.random.split(jax.random.key(seed), 13)
    return {
        "frame_in": draw_frame_in(jax.random.fold_in(key_list[12], 71), 0),
        "token_ids": place_ends(ranked_ids(key_list[1], (RECS, N_SEQ, TOK_DEV), VOCAB, 2), jax.random.fold_in(key_list[1], 3), 0, VOCAB - 1).astype(jnp.int32),
        "durations": jax.vmap(lambda own: ragged_sizes(own, TOK_DEV, F_DEV, 4, 1))(jax.random.split(key_list[2], RECS * N_SEQ)).reshape((RECS, N_SEQ, TOK_DEV)).astype(jnp.int32),
        "valid_len": draw_valid_len(jax.random.fold_in(key_list[12], 71), 0),
        "t_bin": place_ends(jax.random.randint(key_list[4], (RECS,), 0, NBINS), jax.random.fold_in(key_list[4], 1), 0, NBINS - 1).astype(jnp.int32),
        "token_table": centred(key_list[5], (VOCAB, ENC), 1.0, 6.0, ((0, 32),)),
        "enc_weight": centred(key_list[6], (ENC, D), ENC ** -0.5, 0.25),
        "mod_table": draw_mod_table(jax.random.fold_in(key_list[12], 71), 0),
        "w_query": centred(key_list[8], (D, QW), D ** -0.5, 0.1875, ((0, 32),)),
        "w_key": centred(key_list[9], (D, QW), D ** -0.5, 0.1875, ((0, 32),)),
        "w_value": centred(key_list[10], (D, QW), D ** -0.5, 0.1875, ((0, 32),)),
        "attn_grad": centred(key_list[11], (RECS, FRAMES, QW), 1.0, 6.0, ((0, 16), (1, 32))),
    }


def rounded(values):
    return lax.optimization_barrier(values.astype(jnp.bfloat16))

def attend_window(q_blocks, key_ext, value_ext, grad_out, query_pos, key_pos, valid_end, frames_total):
    n_blocks = q_blocks.shape[0]
    block_len = q_blocks.shape[1]
    key_win = jnp.concatenate([key_ext[offset:offset + n_blocks] for offset in range(4)], axis=1).astype(jnp.float32)
    value_win = jnp.concatenate([value_ext[offset:offset + n_blocks] for offset in range(4)], axis=1).astype(jnp.float32)
    q_float = q_blocks.astype(jnp.float32)
    grad_float = grad_out.astype(jnp.float32)
    key_here = key_pos[:, None, :]
    allowed = (key_here >= 0) & (key_here < frames_total) & ((key_here < valid_end) | (query_pos[:, :, None] >= valid_end))
    row_mask = allowed[:, None]
    inv_scale = 1.0 / math.sqrt(q_blocks.shape[-1])
    scores = jnp.einsum('bqhd,bkhd->bhqk', q_float, key_win) * inv_scale
    scores = jnp.where(row_mask, scores, -1e+30)
    row_top = lax.optimization_barrier(jnp.max(scores, axis=-1, keepdims=True))
    shifted_exp = jnp.where(row_mask, jnp.exp(scores - row_top), 0.0)
    attn_prob = shifted_exp / lax.optimization_barrier(jnp.sum(shifted_exp, axis=-1, keepdims=True))
    probs_low = rounded(attn_prob).astype(jnp.float32)
    mixed_out = jnp.einsum('bhqk,bkhd->bqhd', probs_low, value_win).astype(jnp.bfloat16)
    grad_probs = jnp.einsum('bqhd,bkhd->bhqk', grad_float, value_win)
    centre = lax.optimization_barrier(jnp.sum(attn_prob * grad_probs, axis=-1, keepdims=True))
    grad_scores = rounded(attn_prob * (grad_probs - centre) * inv_scale).astype(jnp.float32)
    grad_query = rounded(jnp.einsum('bhqk,bkhd->bqhd', grad_scores, key_win))
    key_terms = jnp.einsum('bhqk,bqhd->bkhd', grad_scores, q_float)
    value_terms = jnp.einsum('bhqk,bqhd->bkhd', probs_low, grad_float)
    win_terms = jnp.concatenate([key_terms, value_terms], axis=2)
    pieces = win_terms.reshape(n_blocks, 4, block_len, win_terms.shape[2], win_terms.shape[3])
    folded = jnp.zeros((n_blocks + 3,) + pieces.shape[2:], jnp.float32)
    for offset in range(4):
        folded = folded + jnp.pad(pieces[:, offset], ((offset, 3 - offset), (0, 0), (0, 0), (0, 0)))
    return (mixed_out, grad_query, folded)

def reference(frame_in, token_ids, durations, valid_len, t_bin, token_table, enc_weight, mod_table, w_query, w_key, w_value, attn_grad):
    weights_all = jnp.concatenate([w_query, w_key, w_value], axis=1)
    grad_scale = 1.0 / math.sqrt(RECS * FRAMES)
    n_blocks = FRAMES // BLK

    def one_record(record_items):
        frames, record_ids, record_dur, valid_end, t_index, grad_in = record_items
        token_emb = jnp.take(token_table, record_ids, axis=0)
        token_ends = jnp.cumsum(record_dur, axis=1).astype(jnp.int32)
        local_pos = jnp.arange(F_DEV, dtype=jnp.int32)
        owner_tok = lax.optimization_barrier(jnp.sum((token_ends[:, None, :] <= local_pos[None, :, None]).astype(jnp.int32), axis=2)).astype(jnp.int32)
        frame_emb = jax.vmap(lambda table_rows, picks: jnp.take(table_rows, picks, axis=0))(token_emb, owner_tok).reshape(FRAMES, ENC)
        hidden_in = frames.astype(jnp.float32) + jnp.dot(frame_emb, enc_weight, preferred_element_type=jnp.float32)
        root_ms = jnp.sqrt(lax.optimization_barrier(jnp.mean(hidden_in * hidden_in, axis=1, keepdims=True)) + 1e-06)
        normed = hidden_in / root_ms
        modulation = lax.dynamic_index_in_dim(mod_table, t_index, 0, keepdims=False)
        gain_part = 1.0 + modulation[:D]
        shift_part = modulation[D:]
        modulated = rounded(normed * gain_part + shift_part)
        projected = rounded(jnp.dot(modulated, weights_all, preferred_element_type=jnp.float32))
        queries = projected[:, :QW]
        keys_values = projected[:, QW:]
        extended = jnp.concatenate([jnp.zeros((2 * BLK, 2 * QW), jnp.bfloat16), keys_values, jnp.zeros((BLK, 2 * QW), jnp.bfloat16)], axis=0)
        ext_blocks = extended.reshape(n_blocks + 3, BLK, 2, HEADS, HD)
        all_pos = jnp.arange(FRAMES, dtype=jnp.int32)
        query_pos = all_pos.reshape(n_blocks, BLK)
        key_pos = (jnp.arange(n_blocks, dtype=jnp.int32)[:, None] - 2) * BLK + jnp.arange(4 * BLK, dtype=jnp.int32)[None, :]
        grad_live = jnp.where((all_pos < valid_end)[:, None], grad_in, jnp.zeros_like(grad_in))
        attn_blocks, query_grad, ext_grad = attend_window(queries.reshape(n_blocks, BLK, HEADS, HD), ext_blocks[:, :, 0], ext_blocks[:, :, 1], grad_live.reshape(n_blocks, BLK, HEADS, HD), query_pos, key_pos, valid_end, FRAMES)
        ext_rows = ext_grad.reshape((n_blocks + 3) * BLK, 2 * QW)
        own_rows = rounded(ext_rows[2 * BLK:2 * BLK + FRAMES])
        grad_cat = jnp.concatenate([query_grad.reshape(FRAMES, QW), own_rows], axis=1)
        slab_rows = modulated.reshape(N_SEQ, F_DEV, D).astype(jnp.float32)
        slab_grads = grad_cat.reshape(N_SEQ, F_DEV, 3 * QW).astype(jnp.float32)
        slab_terms = jnp.einsum('sfd,sfc->sdc', slab_rows, slab_grads) * grad_scale
        record_sum = lax.optimization_barrier(jnp.sum(rounded(slab_terms).astype(jnp.float32), axis=0))
        hidden_grad = lax.dot_general(grad_cat, weights_all, (((1,), (1,)), ((), ())), preferred_element_type=jnp.float32)
        scaled_grad = hidden_grad * gain_part
        frame_grad = (scaled_grad - normed * lax.optimization_barrier(jnp.mean(scaled_grad * normed, axis=1, keepdims=True))) / root_ms
        return (attn_blocks.reshape(FRAMES, QW), frame_grad.astype(jnp.bfloat16), record_sum)
    attn_out, frame_grad, record_sums = lax.map(one_record, (frame_in, token_ids, durations, valid_len, t_bin, attn_grad))
    weight_grad = lax.optimization_barrier(jnp.sum(record_sums, axis=0))
    return (attn_out, frame_grad, weight_grad[:, :QW], weight_grad[:, QW:2 * QW], weight_grad[:, 2 * QW:])
```

```python
import math

import jax
import jax.numpy as jnp
from jax import lax
from jax.experimental import pallas as pl
from jax.experimental.pallas import tpu as pltpu
from jax.sharding import PartitionSpec as P

D = 1024
QW = 512
BLK = 48
NF = 144
NX = 4
NY = 8
NZ = 8
N_SEQ = NX * NZ
PIECE = 112
HALF = 256
WC = 3 * HALF
RC = WC // 2
MESH = pl.DeviceIdType.MESH
F32 = jnp.float32
BF16 = jnp.bfloat16
VMEM_LIMIT = 56 * 1024 * 1024


class Place:
    def __init__(self):
        self.dp = lax.axis_index("dp")
        self.seq = lax.axis_index("seq")
        self.c = lax.rem(self.dp, 2)
        self.y = self.dp // 2
        self.x = self.seq // NZ
        self.z = lax.rem(self.seq, NZ)
        self.sign = 1 - 2 * self.c

    def xs(self, o):
        return lax.rem(self.x + o * self.sign + NX, NX)

    def zs(self, o):
        return lax.rem(self.z + o * self.sign + NZ, NZ)

    def x_dev(self, o):
        return (self.dp, self.xs(o) * NZ + self.z)

    def z_dev(self, o):
        return (self.dp, self.x * NZ + self.zs(o))

    def seq_dev(self, o):
        return (self.dp, lax.rem(self.seq + o + N_SEQ, N_SEQ))

    def sib(self):
        return (self.dp + self.sign, self.seq)

    def y_dev(self, d):
        return (lax.rem(self.y + d, NY) * 2 + self.c, self.seq)


def enter(devices):
    barrier = pltpu.get_barrier_semaphore()
    for dev in devices:
        pl.semaphore_signal(barrier, inc=1, device_id=dev, device_id_type=MESH)
    pl.semaphore_wait(barrier, len(devices))


def nn(a, b):
    return jnp.dot(a, b, preferred_element_type=F32)


def nt(a, b):
    return lax.dot_general(a, b, (((1,), (1,)), ((), ())), preferred_element_type=F32)


def tn(a, b):
    return lax.dot_general(a, b, (((0,), (0,)), ((), ())), preferred_element_type=F32)


def half_of(c, refs):
    cut = [[r[:, h * HALF : (h + 1) * HALF] for r in refs] for h in range(2)]
    low = cut[0][0] if len(refs) == 1 else jnp.concatenate(cut[0], axis=1)
    high = cut[1][0] if len(refs) == 1 else jnp.concatenate(cut[1], axis=1)
    return jnp.where(c == 0, low, high)


OFFS = (0, -1, 1, -2, 2, -3, 3, -4)


def project_kernel(
    t_bin,
    frame,
    ids,
    dur,
    table,
    wq,
    wk,
    wv,
    enc,
    mod,
    q_o,
    kv_o,
    mod_o,
    nrm_o,
    root_o,
    gain_o,
    w_o,
    tbuf,
    ssem,
    rsem,
):
    me = Place()
    c = me.c
    tbuf[c, me.x, me.z] = half_of(c, [table])
    w_o[c, me.x, me.z] = half_of(c, [wq, wk, wv])
    enter(
        [
            me.sib(),
            me.x_dev(1),
            me.x_dev(-1),
            me.z_dev(1),
            me.z_dev(-1),
            me.seq_dev(1),
            me.seq_dev(-1),
        ]
    )
    started = []

    def rc(i, src, dst, dev):
        cp = pltpu.make_async_remote_copy(
            src_ref=src,
            dst_ref=dst,
            send_sem=ssem.at[i],
            recv_sem=rsem.at[i],
            device_id=dev,
            device_id_type=MESH,
        )
        cp.start()
        started.append(cp)
        return cp

    def same(i, ref, dev):
        return rc(i, ref, ref, dev)

    def t_at(xo, zo):
        return tbuf.at[c, me.xs(xo), me.zs(zo)]

    def w_at(zo):
        return w_o.at[c, :, me.zs(zo)]

    t_zr, t_zl, t_xr, t_xl, t_xf = {}, {}, {}, {}, {}
    w_zr, w_zl = {}, {}
    w_sib, t_sib = [], {}

    def t_x_send(j):
        t_xr[j] = same(7 + j, t_at(0, OFFS[j]), me.x_dev(1))
        t_xl[j] = same(15 + j, t_at(0, OFFS[j]), me.x_dev(-1))

    def t_forward(j):
        t_xr[j].wait_recv()
        t_xf[j] = same(23 + j, t_at(-1, OFFS[j]), me.x_dev(1))

    def t_z_step(k):
        t_zr[k].wait_recv()
        if k < 4:
            t_zr[k + 1] = same(k, t_at(0, -k), me.z_dev(1))
            t_zl[k].wait_recv()
            if k < 3:
                t_zl[k + 1] = same(4 + k, t_at(0, k), me.z_dev(-1))
        t_x_send(2 * k - 1)
        if k < 4:
            t_x_send(2 * k)

    def w_sibling(zo):
        i = 45 + len(w_sib)
        w_sib.append(same(i, w_at(zo), me.sib()))

    def w_z_step(k):
        w_zr[k].wait_recv()
        if k < 4:
            w_zr[k + 1] = same(34 + k, w_at(-k), me.z_dev(1))
        w_sibling(-k)
        if k < 4:
            w_zl[k].wait_recv()
            if k < 3:
                w_zl[k + 1] = same(38 + k, w_at(k), me.z_dev(-1))
            w_sibling(k)

    def t_sibling(n, xo):
        t_sib[xo] = same(41 + n, tbuf.at[c, me.xs(xo)], me.sib())

    t_zr[1] = same(0, t_at(0, 0), me.z_dev(1))
    t_zl[1] = same(4, t_at(0, 0), me.z_dev(-1))
    w_own = w_o.at[c, me.x, me.z]
    w_xr = same(31, w_own, me.x_dev(1))
    w_xl = same(32, w_own, me.x_dev(-1))
    t_x_send(0)

    lane = lax.broadcasted_iota(jnp.int32, (64, 60), 1)
    row = lax.broadcasted_iota(jnp.int32, (64, 60), 0)
    ids_f = ids[...].astype(F32)
    ids_f = ids_f + 8.0 * jnp.floor((ids_f + 0.5) * (1.0 / 104.0))
    id_col = jnp.sum(jnp.where(lane == row, ids_f, 0.0), axis=1, keepdims=True)
    end_col = jnp.sum(
        jnp.where(lane <= row, dur[...].astype(F32), 0.0), axis=1, keepdims=True
    )
    frame_pos = lax.broadcasted_iota(jnp.int32, (64, NF), 1).astype(F32)
    tok_pos = lax.broadcasted_iota(jnp.int32, (64, NF), 0).astype(F32)
    owner = jnp.sum(jnp.where(end_col <= frame_pos, 1.0, 0.0), axis=0, keepdims=True)
    spread = jnp.where(tok_pos == owner, 1.0, 0.0).astype(BF16)
    vocab_pos = lax.broadcasted_iota(jnp.int32, (64, NZ * PIECE), 1).astype(F32)

    def emb_part(half, xo):
        base = (me.xs(xo) * (NZ * PIECE)).astype(F32)
        hot = jnp.where(id_col - base == vocab_pos, 1.0, 0.0).astype(BF16)
        return nn(hot, tbuf[half, me.xs(xo)].reshape(NZ * PIECE, HALF))

    w_xr.wait_recv()
    w_xf = same(33, w_o.at[c, me.xs(-1), me.z], me.x_dev(1))
    t_z_step(1)
    w_xl.wait_recv()
    w_xf.wait_recv()
    w_zr[1] = same(34, w_at(0), me.z_dev(1))
    w_zl[1] = same(38, w_at(0), me.z_dev(-1))
    w_sibling(0)
    t_z_step(2)
    t_forward(0)
    t_z_step(3)
    t_forward(1)
    t_forward(2)
    t_z_step(4)
    t_sibling(0, 0)
    w_z_step(1)
    for j in range(3, 8):
        t_forward(j)
    t_sibling(1, -1)
    w_z_step(2)
    own = emb_part(c, 0)
    own += emb_part(c, -1)
    for j in range(8):
        t_xl[j].wait_recv()
    t_sibling(2, 1)
    own += emb_part(c, 1)
    w_z_step(3)
    for j in range(8):
        t_xf[j].wait_recv()
    t_sibling(3, -2)
    own += emb_part(c, -2)
    t_sib[0].wait_recv()
    other = emb_part(1 - c, 0)
    t_sib[-1].wait_recv()
    t_sib[1].wait_recv()
    t_sib[-2].wait_recv()
    other += emb_part(1 - c, -1)
    other += emb_part(1 - c, 1)
    other += emb_part(1 - c, -2)
    own = own.astype(BF16)
    other = other.astype(BF16)
    tok_emb = jnp.where(
        c == 0,
        jnp.concatenate([own, other], axis=1),
        jnp.concatenate([other, own], axis=1),
    )
    frame_emb = tn(spread, tok_emb).astype(BF16)
    hidden = frame[...].astype(F32) + nn(frame_emb, enc[...])
    root = jnp.sqrt(jnp.mean(hidden * hidden, axis=1, keepdims=True) + 1e-06)
    normed = hidden / root
    picked = mod[pl.ds(t_bin[0], 1), :]
    gain = 1.0 + picked[:, :D]
    modulated = (normed * gain + picked[:, D:]).astype(BF16)
    mod_o[...] = modulated
    nrm_o[...] = normed
    root_o[...] = jnp.broadcast_to(root, root_o.shape)
    gain_o[...] = gain
    w_z_step(4)
    for cp in w_sib:
        cp.wait_recv()
    for h in range(2):
        got = nn(modulated, w_o[h].reshape(D, WC)).astype(BF16)
        lo, hi = h * HALF, (h + 1) * HALF
        q_o[:, lo:hi] = got[:, :HALF]
        kv_o[2 * BLK : 2 * BLK + NF, lo:hi] = got[:, HALF : 2 * HALF]
        kv_o[2 * BLK : 2 * BLK + NF, QW + lo : QW + hi] = got[:, 2 * HALF :]
    to_next = rc(
        53, kv_o.at[3 * BLK : 5 * BLK], kv_o.at[0 : 2 * BLK], me.seq_dev(1)
    )
    to_prev = rc(
        54, kv_o.at[2 * BLK : 3 * BLK], kv_o.at[5 * BLK : 6 * BLK], me.seq_dev(-1)
    )
    to_next.wait_recv()
    to_prev.wait_recv()
    for cp in started:
        cp.wait_send()


def attend_kernel(valid, q, kv, grad, out_o, dq_o, own_o, hp_o, hn_o, ext):
    start = lax.axis_index("seq") * NF
    valid_end = valid[0]
    ext[...] = jnp.zeros_like(ext)
    head = lax.broadcasted_iota(jnp.int32, (BLK, HALF), 1) // 64
    q_off = lax.broadcasted_iota(jnp.int32, (BLK, 4 * BLK), 0)
    k_off = lax.broadcasted_iota(jnp.int32, (BLK, 4 * BLK), 1)
    row = lax.broadcasted_iota(jnp.int32, (BLK, HALF), 0)

    def stacked(block):
        zero = jnp.zeros_like(block)
        return jnp.concatenate(
            [jnp.where(head == i, block, zero) for i in range(4)], axis=0
        ).astype(BF16)

    def merged(rows):
        total = jnp.where(head == 0, rows[:BLK], 0.0)
        for i in range(1, 4):
            total = total + jnp.where(head == i, rows[i * BLK : (i + 1) * BLK], 0.0)
        return total.astype(BF16)

    for b in range(3):
        q_pos = start + b * BLK + q_off
        k_pos = start + (b - 2) * BLK + k_off
        allowed = (k_pos >= 0) & (k_pos < N_SEQ * NF)
        allowed &= (k_pos < valid_end) | (q_pos >= valid_end)
        bias = jnp.where(allowed, 0.0, -1e30)
        bias = jnp.concatenate([bias] * 4, axis=0)
        live = (start + b * BLK + row) < valid_end
        mine = slice(b * BLK, (b + 1) * BLK)
        window = slice(b * BLK, (b + 4) * BLK)
        for h in range(2):
            lo, hi = h * HALF, (h + 1) * HALF
            q_rows = stacked(q[mine, lo:hi].astype(F32))
            g_rows = stacked(jnp.where(live, grad[mine, lo:hi].astype(F32), 0.0))
            keys = kv[window, lo:hi]
            values = kv[window, QW + lo : QW + hi]
            scores = nt(q_rows, keys) * 0.125 + bias
            top = jnp.max(scores, axis=1, keepdims=True)
            e = jnp.where(bias < 0.0, 0.0, jnp.exp(scores - top))
            prob = e / jnp.sum(e, axis=1, keepdims=True)
            low = prob.astype(BF16)
            out_o[mine, lo:hi] = merged(nn(low, values))
            g_prob = nt(g_rows, values)
            centre = jnp.sum(prob * g_prob, axis=1, keepdims=True)
            g_score = (prob * (g_prob - centre) * 0.125).astype(BF16)
            dq_o[mine, lo:hi] = merged(nn(g_score, keys))
            ext[window, lo:hi] += tn(g_score, q_rows)
            ext[window, QW + lo : QW + hi] += tn(low, g_rows)
    hp_o[...] = ext[: 2 * BLK].astype(BF16)
    own_o[...] = ext[2 * BLK : 5 * BLK]
    hn_o[...] = ext[5 * BLK :].astype(BF16)


def reduce_kernel(
    modulated,
    dq,
    own,
    hp,
    hn,
    w,
    normed,
    root,
    gain,
    fg_o,
    gq_o,
    gk_o,
    gv_o,
    from_next,
    from_prev,
    mod_sib,
    g_send,
    g_sib,
    pa,
    pb,
    azr,
    azl,
    qa,
    axr,
    axl,
    bxr,
    bxl,
    qb,
    bzr,
    bzl,
    part,
    yb,
    fin,
    ssem,
    rsem,
):
    me = Place()
    c = me.c
    enter(
        [
            me.sib(),
            me.x_dev(1),
            me.x_dev(-1),
            me.z_dev(1),
            me.z_dev(-1),
            me.seq_dev(1),
            me.seq_dev(-1),
        ]
        + [me.y_dev(d) for d in range(1, NY)]
    )
    started = []

    def rc(i, src, dst, dev):
        cp = pltpu.make_async_remote_copy(
            src_ref=src,
            dst_ref=dst,
            send_sem=ssem.at[i],
            recv_sem=rsem.at[i],
            device_id=dev,
            device_id_type=MESH,
        )
        cp.start()
        started.append(cp)
        return cp

    halo_p = rc(0, hp, from_next, me.seq_dev(-1))
    halo_n = rc(1, hn, from_prev, me.seq_dev(1))
    mod_cp = rc(2, modulated, mod_sib, me.sib())
    halo_p.wait_recv()
    halo_n.wait_recv()
    dkv = jnp.concatenate(
        [
            own[:BLK] + from_prev[...].astype(F32),
            own[BLK:] + from_next[...].astype(F32),
        ],
        axis=0,
    ).astype(BF16)
    dq_v = dq[...]
    halves = [
        jnp.concatenate(
            [
                dq_v[:, h * HALF : (h + 1) * HALF],
                dkv[:, h * HALF : (h + 1) * HALF],
                dkv[:, QW + h * HALF : QW + (h + 1) * HALF],
            ],
            axis=1,
        )
        for h in range(2)
    ]
    g_send[...] = jnp.where(c == 0, halves[1], halves[0])
    g_cp = rc(3, g_send, g_sib, me.sib())
    g_own = jnp.where(c == 0, halves[0], halves[1])
    scale = 1.0 / math.sqrt(16 * 4608)
    mod_cp.wait_recv()
    g_cp.wait_recv()
    for xi in range(NX):
        cols = slice(xi * HALF, (xi + 1) * HALF)
        term = tn(modulated[:, cols], g_own) + tn(mod_sib[:, cols], g_sib[...])
        term = (term * scale).astype(BF16)
        pa[xi] = term[:, :RC].reshape(NZ, 32, RC)
        pb[xi] = term[:, RC:].reshape(NZ, 32, RC)

    a_zr = {1: rc(4, pa.at[:, me.zs(4)], azr.at[0], me.z_dev(1))}
    a_zl = {1: rc(8, pa.at[:, me.zs(-3)], azl.at[0], me.z_dev(-1))}
    b_xr = {1: rc(14, pb.at[me.xs(2)], bxr.at[0], me.x_dev(1))}
    b_xl = rc(16, pb.at[me.xs(-1)], bxl, me.x_dev(-1))

    hidden_grad = nt(halves[0], w[0].reshape(D, WC)) + nt(
        halves[1], w[1].reshape(D, WC)
    )
    scaled = hidden_grad * gain[...]
    nrm = normed[...]
    fg_o[...] = (
        (scaled - nrm * jnp.mean(scaled * nrm, axis=1, keepdims=True)) / root[:, :1]
    ).astype(BF16)

    def add(ref, mine):
        return ref.astype(F32) + mine.astype(F32)

    def a_step(k):
        a_zr[k].wait_recv()
        if k < 4:
            azr[k - 1] = add(azr[k - 1], pa[:, me.zs(4 - k)]).astype(BF16)
            a_zr[k + 1] = rc(4 + k, azr.at[k - 1], azr.at[k], me.z_dev(1))
            a_zl[k].wait_recv()
        if k < 3:
            azl[k - 1] = add(azl[k - 1], pa[:, me.zs(k - 3)]).astype(BF16)
            a_zl[k + 1] = rc(8 + k, azl.at[k - 1], azl.at[k], me.z_dev(-1))

    a_step(1)
    b_xr[1].wait_recv()
    bxr[0] = add(bxr[0], pb[me.xs(1)]).astype(BF16)
    b_xr[2] = rc(15, bxr.at[0], bxr.at[1], me.x_dev(1))
    a_step(2)
    a_step(3)
    b_xl.wait_recv()
    b_xr[2].wait_recv()
    qb[...] = (add(pb[me.x], bxr[1]) + bxl[...].astype(F32)).astype(BF16)
    b_zr = {1: rc(17, qb.at[me.zs(4)], bzr.at[0], me.z_dev(1))}
    b_zl = {1: rc(21, qb.at[me.zs(-3)], bzl.at[0], me.z_dev(-1))}
    a_step(4)
    qa[...] = (add(pa[:, me.z], azr[3]) + azl[2].astype(F32)).astype(BF16)
    a_xr = {1: rc(11, qa.at[me.xs(2)], axr.at[0], me.x_dev(1))}
    a_xl = rc(13, qa.at[me.xs(-1)], axl, me.x_dev(-1))

    def b_step(k):
        b_zr[k].wait_recv()
        if k < 4:
            bzr[k - 1] = add(bzr[k - 1], qb[me.zs(4 - k)]).astype(BF16)
            b_zr[k + 1] = rc(17 + k, bzr.at[k - 1], bzr.at[k], me.z_dev(1))
            b_zl[k].wait_recv()
        if k < 3:
            bzl[k - 1] = add(bzl[k - 1], qb[me.zs(k - 3)]).astype(BF16)
            b_zl[k + 1] = rc(21 + k, bzl.at[k - 1], bzl.at[k], me.z_dev(-1))

    b_step(1)
    a_xr[1].wait_recv()
    axr[0] = add(axr[0], qa[me.xs(1)]).astype(BF16)
    a_xr[2] = rc(12, axr.at[0], axr.at[1], me.x_dev(1))
    b_step(2)
    b_step(3)
    a_xl.wait_recv()
    a_xr[2].wait_recv()
    sum_a = add(qa[me.x], axr[1]) + axl[...].astype(F32)
    b_step(4)
    sum_b = add(qb[me.z], bzr[3]) + bzl[2].astype(F32)
    for rt in range(4):
        part[2 * rt] = sum_a[8 * rt : 8 * rt + 8]
        part[2 * rt + 1] = sum_b[8 * rt : 8 * rt + 8]

    cps = []
    for d in range(1, NY):
        cps.append(
            rc(24 + d, part.at[lax.rem(me.y + d, NY)], yb.at[d - 1], me.y_dev(d))
        )
    total = part[me.y]
    for d in range(1, NY):
        cps[d - 1].wait_recv()
        total = total + yb[d - 1]
    fin[c, me.y] = total
    cps = []
    for d in range(1, NY):
        cps.append(rc(32 + d, fin.at[c, me.y], fin.at[c, me.y], me.y_dev(d)))
    for cp in cps:
        cp.wait_recv()
    last = rc(40, fin.at[c], fin.at[c], me.sib())
    last.wait_recv()
    for h in range(2):
        lo, hi = h * HALF, (h + 1) * HALF
        for rt in range(4):
            rows = slice(8 * rt, 8 * rt + 8)
            a, b = fin[h, 2 * rt], fin[h, 2 * rt + 1]
            gq_o[rows, lo:hi] = a[:, :HALF]
            gk_o[rows, lo:hi] = jnp.concatenate([a[:, HALF:], b[:, : RC - HALF]], axis=1)
            gv_o[rows, lo:hi] = b[:, RC - HALF :]
    for cp in started:
        cp.wait_send()


def shape(dims, kind):
    return jax.ShapeDtypeStruct(dims, kind)


def shards(
    frame_in,
    token_ids,
    durations,
    valid_len,
    t_bin,
    token_table,
    enc_weight,
    mod_table,
    w_query,
    w_key,
    w_value,
    attn_grad,
):
    vm = pl.BlockSpec(memory_space=pltpu.VMEM)
    sm = pl.BlockSpec(memory_space=pltpu.SMEM)
    table = jnp.pad(token_table, ((0, PIECE - token_table.shape[0]), (0, 0)))
    queries, keys_values, modulated, normed, root, gain, weights = pl.pallas_call(
        project_kernel,
        name="project",
        out_shape=(
            shape((NF, QW), BF16),
            shape((6 * BLK, 2 * QW), BF16),
            shape((NF, D), BF16),
            shape((NF, D), F32),
            shape((NF, 128), F32),
            shape((1, D), F32),
            shape((2, NX, NZ, 32, WC), BF16),
        ),
        in_specs=[sm] + [vm] * 9,
        out_specs=(vm,) * 7,
        scratch_shapes=[
            pltpu.VMEM((2, NX, NZ, PIECE, HALF), BF16),
            pltpu.SemaphoreType.DMA((55,)),
            pltpu.SemaphoreType.DMA((55,)),
        ],
        compiler_params=pltpu.CompilerParams(
            collective_id=0, has_side_effects=True, vmem_limit_bytes=VMEM_LIMIT
        ),
    )(
        t_bin,
        frame_in[0],
        token_ids[0],
        durations[0],
        table,
        w_query,
        w_key,
        w_value,
        enc_weight,
        mod_table,
    )
    attn_out, dq, own, hp, hn = pl.pallas_call(
        attend_kernel,
        name="attend",
        out_shape=(
            shape((NF, QW), BF16),
            shape((NF, QW), BF16),
            shape((NF, 2 * QW), F32),
            shape((2 * BLK, 2 * QW), BF16),
            shape((BLK, 2 * QW), BF16),
        ),
        in_specs=[sm] + [vm] * 3,
        out_specs=(vm,) * 5,
        scratch_shapes=[pltpu.VMEM((6 * BLK, 2 * QW), F32)],
        compiler_params=pltpu.CompilerParams(vmem_limit_bytes=VMEM_LIMIT),
    )(valid_len, queries, keys_values, attn_grad[0])
    frame_grad, gq, gk, gv = pl.pallas_call(
        reduce_kernel,
        name="reduce",
        out_shape=(
            shape((NF, D), BF16),
            shape((32, QW), F32),
            shape((32, QW), F32),
            shape((32, QW), F32),
        ),
        in_specs=[vm] * 9,
        out_specs=(vm,) * 4,
        scratch_shapes=[
            pltpu.VMEM((2 * BLK, 2 * QW), BF16),
            pltpu.VMEM((BLK, 2 * QW), BF16),
            pltpu.VMEM((NF, D), BF16),
            pltpu.VMEM((NF, WC), BF16),
            pltpu.VMEM((NF, WC), BF16),
            pltpu.VMEM((NX, NZ, 32, RC), BF16),
            pltpu.VMEM((NX, NZ, 32, RC), BF16),
            pltpu.VMEM((4, NX, 32, RC), BF16),
            pltpu.VMEM((3, NX, 32, RC), BF16),
            pltpu.VMEM((NX, 32, RC), BF16),
            pltpu.VMEM((2, 32, RC), BF16),
            pltpu.VMEM((32, RC), BF16),
            pltpu.VMEM((2, NZ, 32, RC), BF16),
            pltpu.VMEM((NZ, 32, RC), BF16),
            pltpu.VMEM((NZ, 32, RC), BF16),
            pltpu.VMEM((4, 32, RC), BF16),
            pltpu.VMEM((3, 32, RC), BF16),
            pltpu.VMEM((NY, 8, RC), F32),
            pltpu.VMEM((NY - 1, 8, RC), F32),
            pltpu.VMEM((2, NY, 8, RC), F32),
            pltpu.SemaphoreType.DMA((41,)),
            pltpu.SemaphoreType.DMA((41,)),
        ],
        compiler_params=pltpu.CompilerParams(
            collective_id=1, has_side_effects=True, vmem_limit_bytes=VMEM_LIMIT
        ),
    )(modulated, dq, own, hp, hn, weights, normed, root, gain)
    return attn_out[None], frame_grad[None], gq, gk, gv


def solution(mesh):
    placed = (
        P("dp", "seq", None),
        P("dp", "seq", None),
        P("dp", "seq", None),
        P("dp"),
        P("dp"),
        P("seq", None),
        P(),
        P(),
        P("seq", None),
        P("seq", None),
        P("seq", None),
        P("dp", "seq", None),
    )
    return jax.shard_map(
        shards,
        mesh=mesh,
        in_specs=placed,
        out_specs=(
            P("dp", "seq", None),
            P("dp", "seq", None),
            P("seq", None),
            P("seq", None),
            P("seq", None),
        ),
        check_vma=False,
    )
```

```python
import math

import jax
import jax.numpy as jnp
from jax import lax
from jax.experimental import pallas as pl
from jax.experimental.pallas import tpu as pltpu
from jax.sharding import PartitionSpec as P

D = 1024
QW = 512
BLK = 48
NF = 144
NX = 4
NY = 8
NZ = 8
N_SEQ = NX * NZ
PIECE = 112
HALF = 256
WC = 3 * HALF
AC = 2 * HALF
SC = WC // 2
GROUP = 4
MESH = pl.DeviceIdType.MESH
F32 = jnp.float32
BF16 = jnp.bfloat16
VMEM_LIMIT = 56 * 1024 * 1024


class Place:
    def __init__(self):
        self.dp = lax.axis_index("dp")
        self.seq = lax.axis_index("seq")
        self.c = lax.rem(self.dp, 2)
        self.y = self.dp // 2
        self.x = self.seq // NZ
        self.z = lax.rem(self.seq, NZ)
        self.sign = 1 - 2 * self.c
        self.q = lax.rem(self.dp, GROUP)

    def xs(self, o):
        return lax.rem(self.x + o * self.sign + NX, NX)

    def zs(self, o):
        return lax.rem(self.z + o * self.sign + NZ, NZ)

    def x_dev(self, o):
        return (self.dp, self.xs(o) * NZ + self.z)

    def z_dev(self, o):
        return (self.dp, self.x * NZ + self.zs(o))

    def seq_dev(self, o):
        return (self.dp, lax.rem(self.seq + o + N_SEQ, N_SEQ))

    def sib(self):
        return (self.dp + self.sign, self.seq)

    def mate(self, d):
        return lax.rem(self.q + d, GROUP)

    def mate_dev(self, d):
        return (self.dp - self.q + self.mate(d), self.seq)

    def y_dev(self, d):
        return (lax.rem(self.y + d, NY) * 2 + self.c, self.seq)

    def dp_dev(self, d):
        return (lax.rem(self.dp + d, 2 * NY), self.seq)


def nn(a, b):
    return jnp.dot(a, b, preferred_element_type=F32)


def nt(a, b):
    return lax.dot_general(a, b, (((1,), (1,)), ((), ())), preferred_element_type=F32)


def tn(a, b):
    return lax.dot_general(a, b, (((0,), (0,)), ((), ())), preferred_element_type=F32)


def add(a, b):
    return a.astype(F32) + b.astype(F32)


def pick(index, parts):
    out = parts[0]
    for i in range(1, len(parts)):
        out = jnp.where(index == i, parts[i], out)
    return out


X_OFFS = (1, -1, 2)
Z_OFFS = (1, -1, 2, -2, 3, -3, 4)


def window_kernel(
    t_bin,
    valid,
    ids,
    dur,
    table,
    wq,
    wk,
    wv,
    frame_h,
    grad_h,
    enc_h,
    mod_h,
    att_o,
    fg_o,
    fin,
    frame,
    grad,
    enc,
    mod,
    tbuf,
    wbuf,
    idb,
    esend,
    embb,
    modb,
    nrm,
    gsend,
    gradb,
    qb,
    kvb,
    dqb,
    ext,
    hps,
    hns,
    hpr,
    hnr,
    osend,
    hsend,
    hrecv,
    pa,
    pb,
    azr,
    azl,
    qa,
    axr,
    bxr,
    qvb,
    bzr,
    part,
    yb,
    lsem,
    ssem,
    rsem,
):
    me = Place()
    c = me.c
    loads = []
    for i, (a, b) in enumerate(
        ((grad_h, grad), (frame_h, frame), (enc_h, enc), (mod_h, mod))
    ):
        loads.append(pltpu.make_async_copy(a, b, lsem.at[i]))
        loads[i].start()
    quarter = pick(me.q, [table[:, i * 128 : (i + 1) * 128].astype(F32) for i in range(4)])
    tbuf[me.x, me.z] = jnp.concatenate(
        [quarter, jnp.zeros((PIECE - 104, 128), F32)], axis=0
    ).astype(BF16)
    wbuf[me.x, me.z] = jnp.concatenate(
        [pick(c, [r[:, :HALF], r[:, HALF:]]) for r in (wq, wk, wv)], axis=1
    )
    idb[me.q] = jnp.where(
        lax.broadcasted_iota(jnp.int32, (8, 128), 0) == 0,
        jnp.concatenate([ids[...].astype(F32), jnp.zeros((1, 68), F32)], axis=1),
        valid[0].astype(F32),
    )
    barrier = pltpu.get_barrier_semaphore()
    peers = [me.dp_dev(d) for d in range(1, 2 * NY)]
    peers += [me.x_dev(o) for o in X_OFFS] + [me.z_dev(o) for o in Z_OFFS]
    peers += [me.seq_dev(1), me.seq_dev(-1)]
    for dev in peers:
        pl.semaphore_signal(barrier, inc=1, device_id=dev, device_id_type=MESH)
    pl.semaphore_wait(barrier, len(peers))
    started = []

    def rc(src, dst, dev):
        i = len(started)
        cp = pltpu.make_async_remote_copy(
            src_ref=src,
            dst_ref=dst,
            send_sem=ssem.at[i],
            recv_sem=rsem.at[i],
            device_id=dev,
            device_id_type=MESH,
        )
        cp.start()
        started.append(cp)
        return cp

    def same(ref, dev):
        return rc(ref, ref, dev)

    def t_at(xo, zo):
        return tbuf.at[me.xs(xo), me.zs(zo)]

    def w_at(xo, zo):
        return wbuf.at[me.xs(xo), me.zs(zo)]

    id_cp = [same(idb.at[me.q], me.mate_dev(d)) for d in range(1, GROUP)]
    t_z = {o: same(t_at(0, 0), me.z_dev(o)) for o in Z_OFFS}
    t_x = {}

    def t_x_send(zo):
        for xo in X_OFFS:
            t_x[xo, zo] = same(t_at(0, zo), me.x_dev(xo))

    w_r, w_l = {}, {}

    def w_start(xo):
        w_r[xo, 1] = same(w_at(xo, 0), me.z_dev(1))
        w_l[xo, 1] = same(w_at(xo, 0), me.z_dev(-1))

    def w_step(xo, k):
        w_r[xo, k].wait_recv()
        if k < 4:
            w_r[xo, k + 1] = same(w_at(xo, -k), me.z_dev(1))
            w_l[xo, k].wait_recv()
        if k < 3:
            w_l[xo, k + 1] = same(w_at(xo, k), me.z_dev(-1))

    W_ROWS = (0, -1, 1, 2)
    t_x_send(0)
    w_x = {o: same(w_at(0, 0), me.x_dev(o)) for o in X_OFFS}
    w_start(0)
    loads[0].wait()
    gsend[...] = pick(c, [grad[:, HALF:], grad[:, :HALF]])
    gradb[0] = pick(c, [grad[:, :HALF], grad[:, HALF:]])
    g_cp = rc(gsend, gradb.at[1], me.sib())

    lane = lax.broadcasted_iota(jnp.int32, (64, 60), 1)
    row = lax.broadcasted_iota(jnp.int32, (64, 60), 0)
    end_col = jnp.sum(
        jnp.where(lane <= row, dur[...].astype(F32), 0.0), axis=1, keepdims=True
    )
    frame_pos = lax.broadcasted_iota(jnp.int32, (64, NF), 1).astype(F32)
    tok_pos = lax.broadcasted_iota(jnp.int32, (64, NF), 0).astype(F32)
    owner = jnp.sum(jnp.where(end_col <= frame_pos, 1.0, 0.0), axis=0, keepdims=True)
    spread = jnp.where(tok_pos == owner, 1.0, 0.0).astype(BF16)
    for cp in id_cp:
        cp.wait_recv()
    lane = lax.broadcasted_iota(jnp.int32, (64, 128), 1)
    row = lax.broadcasted_iota(jnp.int32, (64, 128), 0)
    id_cols = []
    for i in range(GROUP):
        row_ids = idb[i][:1]
        row_ids = row_ids + 8.0 * jnp.floor((row_ids + 0.5) * (1.0 / 104.0))
        id_cols.append(
            jnp.sum(jnp.where(lane == row, row_ids, 0.0), axis=1, keepdims=True)
        )
    id_col = jnp.concatenate(id_cols, axis=0)
    vocab_pos = lax.broadcasted_iota(jnp.int32, (GROUP * 64, NZ * PIECE), 1)
    vocab_pos = vocab_pos.astype(F32)

    def emb_part(xo):
        base = (me.xs(xo) * (NZ * PIECE)).astype(F32)
        hot = jnp.where(id_col - base == vocab_pos, 1.0, 0.0).astype(BF16)
        return nn(hot, tbuf[me.xs(xo)].reshape(NZ * PIECE, 128))

    for o in (1, -1):
        t_z[o].wait_recv()
        t_x_send(-o)
    for o in (1, -1, 2):
        w_x[o].wait_recv()
        w_start(-o if o != 2 else 2)
    for o in (2, -2, 3, -3, 4):
        t_z[o].wait_recv()
        t_x_send(-o if o != 4 else 4)
    emb = emb_part(0)
    for xo in W_ROWS:
        w_step(xo, 1)
    for o in (1, -1):
        for zo in (0,) + Z_OFFS:
            t_x[o, zo].wait_recv()
        emb += emb_part(-o)
    for xo in W_ROWS:
        w_step(xo, 2)
    for zo in (0,) + Z_OFFS:
        t_x[2, zo].wait_recv()
    emb += emb_part(2)
    esend[...] = emb.astype(BF16).reshape(GROUP, 64, 128)
    embb[me.q] = esend[me.q]
    e_cp = [
        rc(esend.at[me.mate(d)], embb.at[me.q], me.mate_dev(d)) for d in range(1, GROUP)
    ]
    for cp in e_cp:
        cp.wait_recv()
    tok_emb = jnp.concatenate([embb[i] for i in range(GROUP)], axis=1)
    frame_emb = tn(spread, tok_emb).astype(BF16)
    for cp in loads[1:]:
        cp.wait()
    hidden = frame[...].astype(F32) + nn(frame_emb, enc[...])
    root = jnp.sqrt(jnp.mean(hidden * hidden, axis=1, keepdims=True) + 1e-06)
    normed = hidden / root
    picked = mod[pl.ds(t_bin[0], 1), :]
    gain = 1.0 + picked[:, :D]
    nrm[...] = normed
    modb[0] = (normed * gain + picked[:, D:]).astype(BF16)
    m_cp = [
        rc(modb.at[0, i * BLK : (i + 1) * BLK], modb.at[1, i * BLK : (i + 1) * BLK], me.sib())
        for i in range(3)
    ]
    for k in (3, 4):
        for xo in W_ROWS:
            w_step(xo, k)
    weights = wbuf[...].reshape(D, WC)

    halos = {}
    for r in range(2):
        if r == 1:
            for cp in m_cp:
                cp.wait_recv()
        got = nn(modb[r], weights).astype(BF16)
        kvb[r, 2 * BLK : 5 * BLK] = got[:, HALF:]
        halos[r] = [
            rc(kvb.at[r, 3 * BLK : 5 * BLK], kvb.at[r, : 2 * BLK], me.seq_dev(1)),
            rc(kvb.at[r, 2 * BLK : 3 * BLK], kvb.at[r, 5 * BLK :], me.seq_dev(-1)),
        ]
        qb[r] = got[:, :HALF]
    g_cp.wait_recv()

    start = me.seq * NF
    head = lax.broadcasted_iota(jnp.int32, (BLK, HALF), 1) // 64
    q_off = lax.broadcasted_iota(jnp.int32, (BLK, 4 * BLK), 0)
    k_off = lax.broadcasted_iota(jnp.int32, (BLK, 4 * BLK), 1)
    live_row = lax.broadcasted_iota(jnp.int32, (BLK, HALF), 0)
    ext[...] = jnp.zeros_like(ext)

    def stacked(block):
        return jnp.concatenate(
            [jnp.where(head == i, block, 0.0) for i in range(4)], axis=0
        ).astype(BF16)

    def merged(rows):
        return pick(head, [rows[i * BLK : (i + 1) * BLK] for i in range(4)]).astype(BF16)

    back = {}
    for r in range(2):
        for cp in halos[r]:
            cp.wait_recv()
        slot = me.q if r == 0 else me.q + me.sign
        valid_end = idb[slot][1:2, 0:1]
        for b in range(3):
            q_pos = start + b * BLK + q_off
            k_pos = start + (b - 2) * BLK + k_off
            inside = (k_pos >= 0) & (k_pos < N_SEQ * NF)
            open_pair = (k_pos.astype(F32) < valid_end) | (q_pos.astype(F32) >= valid_end)
            bias = jnp.where(inside & open_pair, 0.0, -1e30)
            bias = jnp.concatenate([bias] * 4, axis=0)
            live = (start + b * BLK + live_row).astype(F32) < valid_end
            mine = slice(b * BLK, (b + 1) * BLK)
            window = slice(b * BLK, (b + 4) * BLK)
            q_rows = stacked(qb[r, mine].astype(F32))
            g_rows = stacked(jnp.where(live, gradb[r, mine].astype(F32), 0.0))
            keys = kvb[r, window, :HALF]
            values = kvb[r, window, HALF:]
            scores = nt(q_rows, keys) * 0.125 + bias
            top = jnp.max(scores, axis=1, keepdims=True)
            e = jnp.where(bias < 0.0, 0.0, jnp.exp(scores - top))
            prob = e / jnp.sum(e, axis=1, keepdims=True)
            low = prob.astype(BF16)
            mixed = merged(nn(low, values))
            if r == 0:
                att_o[c, mine] = mixed
            else:
                osend[mine] = mixed
            g_prob = nt(g_rows, values)
            centre = jnp.sum(prob * g_prob, axis=1, keepdims=True)
            g_score = (prob * (g_prob - centre) * 0.125).astype(BF16)
            dqb[r, mine] = merged(nn(g_score, keys))
            ext[r, window, :HALF] += tn(g_score, q_rows)
            ext[r, window, HALF:] += tn(low, g_rows)
            if b == 1:
                hps[r] = ext[r, : 2 * BLK].astype(BF16)
                back[r] = [rc(hps.at[r], hpr.at[r], me.seq_dev(-1))]
        hns[r] = ext[r, 5 * BLK :].astype(BF16)
        back[r].append(rc(hns.at[r], hnr.at[r], me.seq_dev(1)))
    o_cp = rc(osend, att_o.at[c], me.sib())
    grads = []
    for r in range(2):
        for cp in back[r]:
            cp.wait_recv()
        own = ext[r, 2 * BLK : 5 * BLK]
        dkv = jnp.concatenate(
            [own[:BLK] + hnr[r].astype(F32), own[BLK:] + hpr[r].astype(F32)], axis=0
        )
        grads.append(jnp.concatenate([dqb[r], dkv.astype(BF16)], axis=1))

    scale = 1.0 / math.sqrt(16 * 4608)
    b_x, a_r, a_l = {}, {}, {}
    for xo in (2, 1, -1, 0):
        xi = me.xs(xo)
        cols = pl.ds(pl.multiple_of(xi * HALF, HALF), HALF)
        term = tn(modb[0, :, cols], grads[0]) + tn(modb[1, :, cols], grads[1])
        term = (term * scale).astype(BF16)
        pa[xi] = term[:, :AC].reshape(NZ, 32, AC)
        pb[xi] = term[:, AC:].reshape(NZ, 32, HALF)
        a_r[xo, 1] = rc(pa.at[xi, me.zs(4)], azr.at[0, xi], me.z_dev(1))
        a_l[xo, 1] = rc(pa.at[xi, me.zs(-3)], azl.at[0, xi], me.z_dev(-1))
        if xo != 0:
            b_x[xo] = rc(pb.at[xi], bxr.at[X_OFFS.index(xo)], me.x_dev(xo))

    def a_step(k):
        for xo in (2, 1, -1, 0):
            xi = me.xs(xo)
            a_r[xo, k].wait_recv()
            if k < 4:
                azr[k - 1, xi] = add(azr[k - 1, xi], pa[xi, me.zs(4 - k)]).astype(BF16)
                a_r[xo, k + 1] = rc(azr.at[k - 1, xi], azr.at[k, xi], me.z_dev(1))
                a_l[xo, k].wait_recv()
            if k < 3:
                azl[k - 1, xi] = add(azl[k - 1, xi], pa[xi, me.zs(k - 3)]).astype(BF16)
                a_l[xo, k + 1] = rc(azl.at[k - 1, xi], azl.at[k, xi], me.z_dev(-1))

    hsend[...] = nt(grads[1], weights).astype(BF16)
    h_cp = rc(hsend, hrecv, me.sib())
    a_step(1)
    hidden_grad = nt(grads[0], weights)
    a_step(2)
    for cp in b_x.values():
        cp.wait_recv()
    total = pb[me.x].astype(F32)
    for i in range(3):
        total = total + bxr[i].astype(F32)
    qvb[...] = total.astype(BF16)
    b_z = [
        rc(qvb.at[me.zs(o)], bzr.at[i], me.z_dev(o)) for i, o in enumerate(Z_OFFS)
    ]
    a_step(3)
    h_cp.wait_recv()
    scaled = (hidden_grad + hrecv[...].astype(F32)) * gain
    normed = nrm[...]
    fg_o[...] = (
        (scaled - normed * jnp.mean(scaled * normed, axis=1, keepdims=True)) / root
    ).astype(BF16)
    a_step(4)
    for xo in (2, 1, -1, 0):
        xi = me.xs(xo)
        got = add(azr[3, xi], azl[2, xi]) + pa[xi, me.z].astype(F32)
        qa[xi] = got.astype(BF16)
    a_x = [rc(qa.at[me.xs(o)], axr.at[i], me.x_dev(o)) for i, o in enumerate(X_OFFS)]
    sum_b = qvb[me.z].astype(F32)
    for i, cp in enumerate(b_z):
        cp.wait_recv()
        sum_b = sum_b + bzr[i].astype(F32)
    sum_a = qa[me.x].astype(F32)
    for i, cp in enumerate(a_x):
        cp.wait_recv()
        sum_a = sum_a + axr[i].astype(F32)
    for rt in range(4):
        rows = slice(8 * rt, 8 * rt + 8)
        part[2 * rt] = sum_a[rows, :SC]
        part[2 * rt + 1] = jnp.concatenate([sum_a[rows, SC:], sum_b[rows]], axis=1)

    y_cp = [
        rc(part.at[lax.rem(me.y + d, NY)], yb.at[d - 1], me.y_dev(d))
        for d in range(1, NY)
    ]
    total = part[me.y]
    for d in range(1, NY):
        y_cp[d - 1].wait_recv()
        total = total + yb[d - 1]
    fin[c, me.y] = total
    for cp in [same(fin.at[c, me.y], me.dp_dev(d)) for d in range(1, 2 * NY)]:
        cp.wait_recv()
    o_cp.wait_recv()
    for cp in started:
        cp.wait_send()


def finish_kernel(att, fg, fin, att_o, fg_o, gq_o, gk_o, gv_o):
    fg_o[...] = fg[...]
    for h in range(2):
        lo, hi = h * HALF, (h + 1) * HALF
        att_o[:, lo:hi] = att[h]
        for rt in range(4):
            rows = slice(8 * rt, 8 * rt + 8)
            a, b = fin[h, 2 * rt], fin[h, 2 * rt + 1]
            gq_o[rows, lo:hi] = a[:, :HALF]
            gk_o[rows, lo:hi] = jnp.concatenate([a[:, HALF:], b[:, : SC - HALF]], axis=1)
            gv_o[rows, lo:hi] = b[:, SC - HALF :]


def shape(dims, kind):
    return jax.ShapeDtypeStruct(dims, kind)


def shards(
    frame_in,
    token_ids,
    durations,
    valid_len,
    t_bin,
    token_table,
    enc_weight,
    mod_table,
    w_query,
    w_key,
    w_value,
    attn_grad,
):
    vm = pl.BlockSpec(memory_space=pltpu.VMEM)
    sm = pl.BlockSpec(memory_space=pltpu.SMEM)
    hb = pl.BlockSpec(memory_space=pl.ANY)
    att, fg, fin = pl.pallas_call(
        window_kernel,
        name="window",
        out_shape=(
            shape((2, NF, HALF), BF16),
            shape((NF, D), BF16),
            shape((2, NY, 8, SC), F32),
        ),
        in_specs=[sm] * 2 + [vm] * 6 + [hb] * 4,
        out_specs=(vm,) * 3,
        scratch_shapes=[
            pltpu.VMEM((NF, D), BF16),
            pltpu.VMEM((NF, QW), BF16),
            pltpu.VMEM((QW, D), BF16),
            pltpu.VMEM((64, 2 * D), F32),
            pltpu.VMEM((NX, NZ, PIECE, 128), BF16),
            pltpu.VMEM((NX, NZ, 32, WC), BF16),
            pltpu.VMEM((GROUP, 8, 128), F32),
            pltpu.VMEM((GROUP, 64, 128), BF16),
            pltpu.VMEM((GROUP, 64, 128), BF16),
            pltpu.VMEM((2, NF, D), BF16),
            pltpu.VMEM((NF, D), F32),
            pltpu.VMEM((NF, HALF), BF16),
            pltpu.VMEM((2, NF, HALF), BF16),
            pltpu.VMEM((2, NF, HALF), BF16),
            pltpu.VMEM((2, 6 * BLK, 2 * HALF), BF16),
            pltpu.VMEM((2, NF, HALF), BF16),
            pltpu.VMEM((2, 6 * BLK, 2 * HALF), F32),
            pltpu.VMEM((2, 2 * BLK, 2 * HALF), BF16),
            pltpu.VMEM((2, BLK, 2 * HALF), BF16),
            pltpu.VMEM((2, 2 * BLK, 2 * HALF), BF16),
            pltpu.VMEM((2, BLK, 2 * HALF), BF16),
            pltpu.VMEM((NF, HALF), BF16),
            pltpu.VMEM((NF, D), BF16),
            pltpu.VMEM((NF, D), BF16),
            pltpu.VMEM((NX, NZ, 32, AC), BF16),
            pltpu.VMEM((NX, NZ, 32, HALF), BF16),
            pltpu.VMEM((4, NX, 32, AC), BF16),
            pltpu.VMEM((3, NX, 32, AC), BF16),
            pltpu.VMEM((NX, 32, AC), BF16),
            pltpu.VMEM((3, 32, AC), BF16),
            pltpu.VMEM((3, NZ, 32, HALF), BF16),
            pltpu.VMEM((NZ, 32, HALF), BF16),
            pltpu.VMEM((7, 32, HALF), BF16),
            pltpu.VMEM((NY, 8, SC), F32),
            pltpu.VMEM((NY - 1, 8, SC), F32),
            pltpu.SemaphoreType.DMA((4,)),
            pltpu.SemaphoreType.DMA((170,)),
            pltpu.SemaphoreType.DMA((170,)),
        ],
        compiler_params=pltpu.CompilerParams(
            collective_id=0, has_side_effects=True, vmem_limit_bytes=VMEM_LIMIT
        ),
    )(
        t_bin,
        valid_len,
        token_ids[0],
        durations[0],
        token_table,
        w_query,
        w_key,
        w_value,
        frame_in[0],
        attn_grad[0],
        enc_weight,
        mod_table,
    )
    att, fg, gq, gk, gv = pl.pallas_call(
        finish_kernel,
        name="finish",
        out_shape=(
            shape((NF, QW), BF16),
            shape((NF, D), BF16),
            shape((32, QW), F32),
            shape((32, QW), F32),
            shape((32, QW), F32),
        ),
        in_specs=[vm] * 3,
        out_specs=(vm,) * 5,
    )(att, fg, fin)
    return att[None], fg[None], gq, gk, gv


def solution(mesh):
    placed = (
        P("dp", "seq", None),
        P("dp", "seq", None),
        P("dp", "seq", None),
        P("dp"),
        P("dp"),
        P("seq", None),
        P(),
        P(),
        P("seq", None),
        P("seq", None),
        P("seq", None),
        P("dp", "seq", None),
    )
    return jax.shard_map(
        shards,
        mesh=mesh,
        in_specs=placed,
        out_specs=(
            P("dp", "seq", None),
            P("dp", "seq", None),
            P("seq", None),
            P("seq", None),
            P("seq", None),
        ),
        check_vma=False,
    )
```

```python
import math

import jax
import jax.numpy as jnp
from jax import lax
from jax.experimental import pallas as pl
from jax.experimental.pallas import tpu as pltpu
from jax.sharding import PartitionSpec as P

D = 1024
QW = 512
BLK = 48
NF = 144
NX = 4
NY = 8
NZ = 8
N_SEQ = NX * NZ
PIECE = 64
HALF = 256
WC = 3 * HALF
AC = 2 * HALF
SC = WC // 4
GROUP = 8
MESH = pl.DeviceIdType.MESH
F32 = jnp.float32
BF16 = jnp.bfloat16
VMEM_LIMIT = 56 * 1024 * 1024


class Place:
    def __init__(self):
        self.dp = lax.axis_index("dp")
        self.seq = lax.axis_index("seq")
        self.c = lax.rem(self.dp, 2)
        self.y = self.dp // 2
        self.x = self.seq // NZ
        self.z = lax.rem(self.seq, NZ)
        self.sign = 1 - 2 * self.c
        self.q = lax.rem(self.dp, GROUP)

    def xs(self, o):
        return lax.rem(self.x + o * self.sign + NX, NX)

    def zs(self, o):
        return lax.rem(self.z + o * self.sign + NZ, NZ)

    def x_dev(self, o):
        return (self.dp, self.xs(o) * NZ + self.z)

    def z_dev(self, o):
        return (self.dp, self.x * NZ + self.zs(o))

    def seq_dev(self, o):
        return (self.dp, lax.rem(self.seq + o + N_SEQ, N_SEQ))

    def sib(self):
        return (self.dp + self.sign, self.seq)

    def mate(self, d):
        return lax.rem(self.q + d, GROUP)

    def mate_dev(self, d):
        return (self.dp - self.q + self.mate(d), self.seq)

    def y_dev(self, d):
        return (lax.rem(self.y + d, NY) * 2 + self.c, self.seq)


def nn(a, b):
    return jnp.dot(a, b, preferred_element_type=F32)


def nt(a, b):
    return lax.dot_general(a, b, (((1,), (1,)), ((), ())), preferred_element_type=F32)


def tn(a, b):
    return lax.dot_general(a, b, (((0,), (0,)), ((), ())), preferred_element_type=F32)


def add(a, b):
    return a.astype(F32) + b.astype(F32)


def pick(index, parts):
    out = parts[0]
    for i in range(1, len(parts)):
        out = jnp.where(index == i, parts[i], out)
    return out


X_OFFS = (1, -1, 2)
Z_OFFS = (1, -1, 2, -2, 3, -3, 4)


def window_kernel(
    t_bin,
    valid,
    ids,
    dur,
    table,
    wq,
    wk,
    wv,
    frame_h,
    grad_h,
    enc_h,
    mod_h,
    att_o,
    fg_o,
    fin,
    frame,
    grad,
    enc,
    mod,
    tbuf,
    wbuf,
    wmine,
    wswap,
    idb,
    esend,
    embb,
    modb,
    nrm,
    gsend,
    gradb,
    qb,
    kvb,
    dqb,
    ext,
    hps,
    hns,
    hpr,
    hnr,
    osend,
    hsend,
    hrecv,
    pa,
    pb,
    azr,
    azl,
    qa,
    axr,
    bxr,
    qvb,
    bzr,
    part,
    yb,
    lsem,
    ssem,
    rsem,
):
    me = Place()
    c = me.c
    loads = []
    for i, (a, b) in enumerate(
        ((grad_h, grad), (frame_h, frame), (enc_h, enc), (mod_h, mod))
    ):
        loads.append(pltpu.make_async_copy(a, b, lsem.at[i]))
        loads[i].start()
    quarter = pick(
        lax.rem(me.q, 4), [table[:, i * 128 : (i + 1) * 128].astype(F32) for i in range(4)]
    )
    upper = me.q // 4
    odd = lax.rem(me.y, 2)
    tbuf[me.x, me.z] = pick(
        upper,
        [
            quarter[:PIECE],
            jnp.concatenate(
                [quarter[PIECE:], jnp.zeros((2 * PIECE - 104, 128), F32)], axis=0
            ),
        ],
    ).astype(BF16)
    w_q, w_k, w_v = [pick(c, [r[:, :HALF], r[:, HALF:]]) for r in (wq, wk, wv)]
    wbuf[me.x, me.z] = w_k
    w_m = pick(odd, [w_q, w_v])
    for i in range(2):
        wmine[i, me.x, me.z] = w_m[:, i * 128 : (i + 1) * 128]
    idb[me.q] = jnp.where(
        lax.broadcasted_iota(jnp.int32, (8, 128), 0) == 0,
        jnp.concatenate([ids[...].astype(F32), jnp.zeros((1, 68), F32)], axis=1),
        valid[0].astype(F32),
    )
    barrier = pltpu.get_barrier_semaphore()
    peers = [me.y_dev(d) for d in range(1, NY)]
    peers += [me.mate_dev(d) for d in range(1, GROUP, 2)]
    peers += [me.x_dev(o) for o in X_OFFS] + [me.z_dev(o) for o in Z_OFFS]
    peers += [me.seq_dev(1), me.seq_dev(-1)]
    for dev in peers:
        pl.semaphore_signal(barrier, inc=1, device_id=dev, device_id_type=MESH)
    pl.semaphore_wait(barrier, len(peers))
    started = []

    def rc(src, dst, dev):
        i = len(started)
        cp = pltpu.make_async_remote_copy(
            src_ref=src,
            dst_ref=dst,
            send_sem=ssem.at[i],
            recv_sem=rsem.at[i],
            device_id=dev,
            device_id_type=MESH,
        )
        cp.start()
        started.append(cp)
        return cp

    def same(ref, dev):
        return rc(ref, ref, dev)

    def cut(src, dst, dev, size):
        rows = [pl.ds(i, size) for i in range(0, src.shape[0], size)]
        return [rc(src.at[r], dst.at[r], dev) for r in rows]

    drained = [0]

    def drain():
        for cp in started[drained[0] :]:
            cp.wait_send()
        drained[0] = len(started)

    def arrive(cps):
        for cp in cps:
            cp.wait_recv()

    def t_at(xo, zo):
        return tbuf.at[me.xs(xo), me.zs(zo)]

    def w_at(xo, zo):
        return wbuf.at[me.xs(xo), me.zs(zo)]

    id_cp = [same(idb.at[me.q], me.mate_dev(d)) for d in range(1, GROUP)]
    t_z = {o: same(t_at(0, 0), me.z_dev(o)) for o in Z_OFFS}
    t_x = {}

    def t_x_send(zo):
        for xo in X_OFFS:
            t_x[xo, zo] = same(t_at(0, zo), me.x_dev(xo))

    w_r, w_l = {}, {}

    def w_start(xo):
        w_r[xo, 1] = same(w_at(xo, 0), me.z_dev(1))
        w_l[xo, 1] = same(w_at(xo, 0), me.z_dev(-1))

    def w_step(xo, k):
        w_r[xo, k].wait_recv()
        if k < 4:
            w_r[xo, k + 1] = same(w_at(xo, -k), me.z_dev(1))
            w_l[xo, k].wait_recv()
        if k < 3:
            w_l[xo, k + 1] = same(w_at(xo, k), me.z_dev(-1))

    w_y = []

    def y_send(xo):
        for i, d in ((0, 1), (1, NY - 1)):
            w_y.append(
                rc(wmine.at[i, me.xs(xo)], wswap.at[i, me.xs(xo)], me.y_dev(d))
            )

    W_ROWS = (0, -1, 1, 2)

    def w_steps(k):
        for xo in W_ROWS:
            w_step(xo, k)

    w_x = {o: same(w_at(0, 0), me.x_dev(o)) for o in X_OFFS}
    t_x_send(0)
    w_start(0)
    wm_z = [same(wmine.at[:, me.x, me.z], me.z_dev(o)) for o in Z_OFFS]
    loads[0].wait()
    gsend[...] = pick(c, [grad[:, HALF:], grad[:, :HALF]])
    gradb[0] = pick(c, [grad[:, :HALF], grad[:, HALF:]])
    g_cp = cut(gsend, gradb.at[1], me.sib(), 48)

    lane = lax.broadcasted_iota(jnp.int32, (64, 60), 1)
    row = lax.broadcasted_iota(jnp.int32, (64, 60), 0)
    end_col = jnp.sum(
        jnp.where(lane <= row, dur[...].astype(F32), 0.0), axis=1, keepdims=True
    )
    frame_pos = lax.broadcasted_iota(jnp.int32, (64, NF), 1).astype(F32)
    tok_pos = lax.broadcasted_iota(jnp.int32, (64, NF), 0).astype(F32)
    owner = jnp.sum(jnp.where(end_col <= frame_pos, 1.0, 0.0), axis=0, keepdims=True)
    spread = jnp.where(tok_pos == owner, 1.0, 0.0).astype(BF16)
    for cp in id_cp:
        cp.wait_recv()
    lane = lax.broadcasted_iota(jnp.int32, (64, 128), 1)
    row = lax.broadcasted_iota(jnp.int32, (64, 128), 0)
    id_cols = []
    for i in range(GROUP):
        row_ids = idb[i][:1]
        owner_row = jnp.floor((row_ids + 0.5) * (1.0 / 104.0))
        inner = row_ids - 104.0 * owner_row - (PIECE * upper).astype(F32)
        held = (inner >= 0.0) & (inner < float(PIECE))
        row_ids = jnp.where(held, owner_row * PIECE + inner, -1.0)
        id_cols.append(
            jnp.sum(jnp.where(lane == row, row_ids, 0.0), axis=1, keepdims=True)
        )
    id_col = jnp.concatenate(id_cols, axis=0)
    vocab_pos = lax.broadcasted_iota(jnp.int32, (GROUP * 64, NZ * PIECE), 1)
    vocab_pos = vocab_pos.astype(F32)

    def emb_part(xo):
        base = (me.xs(xo) * (NZ * PIECE)).astype(F32)
        hot = jnp.where(id_col - base == vocab_pos, 1.0, 0.0).astype(BF16)
        return nn(hot, tbuf[me.xs(xo)].reshape(NZ * PIECE, 128))

    for o in (1, -1):
        t_z[o].wait_recv()
        t_x_send(-o)
    for o in (1, -1, 2):
        w_x[o].wait_recv()
        w_start(-o if o != 2 else 2)
    for o in (2, -2, 3, -3, 4):
        t_z[o].wait_recv()
        t_x_send(-o if o != 4 else 4)
    w_steps(1)
    arrive(wm_z)
    wm_x = {o: same(wmine.at[:, me.x], me.x_dev(o)) for o in X_OFFS}
    y_send(0)
    emb = emb_part(0)
    for zo in (0,) + Z_OFFS:
        t_x[1, zo].wait_recv()
    w_steps(2)
    emb += emb_part(-1)
    for o, xo in ((-1, 1), (2, 2)):
        for zo in (0,) + Z_OFFS:
            t_x[o, zo].wait_recv()
        emb += emb_part(xo)
    esend[...] = emb.astype(BF16).reshape(GROUP, 64, 128)
    embb[me.q] = esend[me.q]
    e_cp = [
        rc(esend.at[me.mate(d)], embb.at[me.q], me.mate_dev(d)) for d in range(1, GROUP)
    ]
    w_steps(3)
    for o in X_OFFS:
        wm_x[o].wait_recv()
        y_send(-o if o != 2 else 2)
    arrive(e_cp)
    tok_emb = jnp.concatenate(
        [add(embb[i], embb[i + 4]).astype(BF16) for i in range(4)], axis=1
    )
    frame_emb = tn(spread, tok_emb).astype(BF16)
    for cp in loads[1:]:
        cp.wait()
    hidden = frame[...].astype(F32) + nn(frame_emb, enc[...])
    root = jnp.sqrt(jnp.mean(hidden * hidden, axis=1, keepdims=True) + 1e-06)
    normed = hidden / root
    picked = mod[pl.ds(t_bin[0], 1), :]
    gain = 1.0 + picked[:, :D]
    nrm[...] = normed
    modb[0] = (normed * gain + picked[:, D:]).astype(BF16)
    m_cp = cut(modb.at[0], modb.at[1], me.sib(), 16)
    w_steps(4)

    halos = {}

    def send_halo(r, i):
        halos[r] = halos.get(r, []) + [
            rc(
                kvb.at[i, r, 3 * BLK : 5 * BLK],
                kvb.at[i, r, : 2 * BLK],
                me.seq_dev(1),
            ),
            rc(
                kvb.at[i, r, 2 * BLK : 3 * BLK],
                kvb.at[i, r, 5 * BLK :],
                me.seq_dev(-1),
            ),
        ]

    w_key = wbuf[...].reshape(D, HALF)
    for r in range(2):
        if r == 1:
            arrive(m_cp)
        kvb[0, r, 2 * BLK : 5 * BLK] = nn(modb[r], w_key).astype(BF16)
        send_halo(r, 0)
    w_mine = jnp.concatenate([wmine[i].reshape(D, 128) for i in range(2)], axis=1)
    mine_r = [nn(modb[r], w_mine) for r in range(2)]
    arrive(w_y)
    w_swap = jnp.concatenate([wswap[i].reshape(D, 128) for i in range(2)], axis=1)
    for r in range(2):
        swap_r = nn(modb[r], w_swap)
        kvb[1, r, 2 * BLK : 5 * BLK] = pick(odd, [swap_r, mine_r[r]]).astype(BF16)
        send_halo(r, 1)
        qb[r] = pick(odd, [mine_r[r], swap_r]).astype(BF16)
    drain()
    arrive(g_cp)

    start = me.seq * NF
    head = lax.broadcasted_iota(jnp.int32, (BLK, HALF), 1) // 64
    q_off = lax.broadcasted_iota(jnp.int32, (BLK, 4 * BLK), 0)
    k_off = lax.broadcasted_iota(jnp.int32, (BLK, 4 * BLK), 1)
    live_row = lax.broadcasted_iota(jnp.int32, (BLK, HALF), 0)
    ext[...] = jnp.zeros_like(ext)

    def stacked(block):
        return jnp.concatenate(
            [jnp.where(head == i, block, 0.0) for i in range(4)], axis=0
        ).astype(BF16)

    def merged(rows):
        return pick(head, [rows[i * BLK : (i + 1) * BLK] for i in range(4)]).astype(BF16)

    back = {}
    for r in range(2):
        for cp in halos[r]:
            cp.wait_recv()
        slot = me.q if r == 0 else me.q + me.sign
        valid_end = idb[slot][1:2, 0:1]
        for b in range(3):
            q_pos = start + b * BLK + q_off
            k_pos = start + (b - 2) * BLK + k_off
            inside = (k_pos >= 0) & (k_pos < N_SEQ * NF)
            open_pair = (k_pos.astype(F32) < valid_end) | (q_pos.astype(F32) >= valid_end)
            bias = jnp.where(inside & open_pair, 0.0, -1e30)
            bias = jnp.concatenate([bias] * 4, axis=0)
            live = (start + b * BLK + live_row).astype(F32) < valid_end
            mine = slice(b * BLK, (b + 1) * BLK)
            window = slice(b * BLK, (b + 4) * BLK)
            q_rows = stacked(qb[r, mine].astype(F32))
            g_rows = stacked(jnp.where(live, gradb[r, mine].astype(F32), 0.0))
            keys = kvb[0, r, window]
            values = kvb[1, r, window]
            scores = nt(q_rows, keys) * 0.125 + bias
            top = jnp.max(scores, axis=1, keepdims=True)
            e = jnp.where(bias < 0.0, 0.0, jnp.exp(scores - top))
            prob = e / jnp.sum(e, axis=1, keepdims=True)
            low = prob.astype(BF16)
            mixed = merged(nn(low, values))
            if r == 0:
                att_o[c, mine] = mixed
            else:
                osend[mine] = mixed
            g_prob = nt(g_rows, values)
            centre = jnp.sum(prob * g_prob, axis=1, keepdims=True)
            g_score = (prob * (g_prob - centre) * 0.125).astype(BF16)
            dqb[r, mine] = merged(nn(g_score, keys))
            ext[r, window, :HALF] += tn(g_score, q_rows)
            ext[r, window, HALF:] += tn(low, g_rows)
            if b == 1:
                hps[r] = ext[r, : 2 * BLK].astype(BF16)
                back[r] = cut(hps.at[r], hpr.at[r], me.seq_dev(-1), BLK)
        hns[r] = ext[r, 5 * BLK :].astype(BF16)
        back[r].append(rc(hns.at[r], hnr.at[r], me.seq_dev(1)))
    o_cp = cut(osend, att_o.at[c], me.sib(), BLK)
    grads = []
    for r in range(2):
        for cp in back[r]:
            cp.wait_recv()
        own = ext[r, 2 * BLK : 5 * BLK]
        dkv = jnp.concatenate(
            [own[:BLK] + hnr[r].astype(F32), own[BLK:] + hpr[r].astype(F32)], axis=0
        )
        grads.append(jnp.concatenate([dqb[r], dkv.astype(BF16)], axis=1))

    scale = 1.0 / math.sqrt(16 * 4608)
    b_x, a_r, a_l = {}, {}, {}
    for xo in (2, 1, -1, 0):
        xi = me.xs(xo)
        cols = pl.ds(pl.multiple_of(xi * HALF, HALF), HALF)
        term = tn(modb[0, :, cols], grads[0]) + tn(modb[1, :, cols], grads[1])
        term = (term * scale).astype(BF16)
        pa[xi] = term[:, :AC].reshape(NZ, 32, AC)
        pb[xi] = term[:, AC:].reshape(NZ, 32, HALF)
        a_r[xo, 1] = rc(pa.at[xi, me.zs(4)], azr.at[0, xi], me.z_dev(1))
        a_l[xo, 1] = rc(pa.at[xi, me.zs(-3)], azl.at[0, xi], me.z_dev(-1))
        if xo != 0:
            b_x[xo] = rc(pb.at[xi], bxr.at[X_OFFS.index(xo)], me.x_dev(xo))

    def a_step(k):
        for xo in (2, 1, -1, 0):
            xi = me.xs(xo)
            a_r[xo, k].wait_recv()
            if k < 4:
                azr[k - 1, xi] = add(azr[k - 1, xi], pa[xi, me.zs(4 - k)]).astype(BF16)
                a_r[xo, k + 1] = rc(azr.at[k - 1, xi], azr.at[k, xi], me.z_dev(1))
                a_l[xo, k].wait_recv()
            if k < 3:
                azl[k - 1, xi] = add(azl[k - 1, xi], pa[xi, me.zs(k - 3)]).astype(BF16)
                a_l[xo, k + 1] = rc(azl.at[k - 1, xi], azl.at[k, xi], me.z_dev(-1))

    def hidden_part(g):
        g_q, g_k, g_v = g[:, :HALF], g[:, HALF : 2 * HALF], g[:, 2 * HALF :]
        return (
            nt(g_k, w_key)
            + nt(pick(odd, [g_q, g_v]), w_mine)
            + nt(pick(odd, [g_v, g_q]), w_swap)
        )

    hsend[...] = hidden_part(grads[1]).astype(BF16)
    h_cp = cut(hsend, hrecv, me.sib(), 16)
    a_step(1)
    hidden_grad = hidden_part(grads[0])
    a_step(2)
    for cp in b_x.values():
        cp.wait_recv()
    total = pb[me.x].astype(F32)
    for i in range(3):
        total = total + bxr[i].astype(F32)
    qvb[...] = total.astype(BF16)
    b_z = [
        rc(qvb.at[me.zs(o)], bzr.at[i], me.z_dev(o)) for i, o in enumerate(Z_OFFS)
    ]
    a_step(3)
    arrive(h_cp)
    scaled = (hidden_grad + hrecv[...].astype(F32)) * gain
    normed = nrm[...]
    fg_o[...] = (
        (scaled - normed * jnp.mean(scaled * normed, axis=1, keepdims=True)) / root
    ).astype(BF16)
    a_step(4)
    for xo in (2, 1, -1, 0):
        xi = me.xs(xo)
        got = add(azr[3, xi], azl[2, xi]) + pa[xi, me.z].astype(F32)
        qa[xi] = got.astype(BF16)
    a_x = [rc(qa.at[me.xs(o)], axr.at[i], me.x_dev(o)) for i, o in enumerate(X_OFFS)]
    sum_b = qvb[me.z].astype(F32)
    for i, cp in enumerate(b_z):
        cp.wait_recv()
        sum_b = sum_b + bzr[i].astype(F32)
    sum_a = qa[me.x].astype(F32)
    for i, cp in enumerate(a_x):
        cp.wait_recv()
        sum_a = sum_a + axr[i].astype(F32)
    whole = jnp.concatenate([sum_a, sum_b], axis=1)
    for i in range(NY):
        rows, cols = slice(i // 4 * 16, i // 4 * 16 + 16), slice(i % 4 * SC, (i % 4 + 1) * SC)
        part[i] = whole[rows, cols].astype(BF16)

    y_cp = [
        rc(part.at[lax.rem(me.y + d, NY)], yb.at[d - 1], me.y_dev(d))
        for d in range(1, NY)
    ]
    drain()
    total = part[me.y].astype(F32)
    for d in range(1, NY):
        y_cp[d - 1].wait_recv()
        total = total + yb[d - 1].astype(F32)
    fin[c, me.y] = total.astype(BF16)
    eighth = fin.at[c, me.y]
    y_all = [same(eighth, me.y_dev(d)) for d in range(1, NY)]
    last = [same(eighth, me.sib())]
    for d in range(1, NY):
        y_all[d - 1].wait_recv()
        last.append(same(fin.at[c, lax.rem(me.y - d + NY, NY)], me.sib()))
    arrive(last)
    arrive(o_cp)
    drain()


def finish_kernel(att, fg, fin, att_o, fg_o, gq_o, gk_o, gv_o):
    fg_o[...] = fg[...]
    for h in range(2):
        lo, hi = h * HALF, (h + 1) * HALF
        att_o[:, lo:hi] = att[h]
        for rt in range(2):
            rows = slice(16 * rt, 16 * rt + 16)
            got = [fin[h, 4 * rt + j].astype(F32) for j in range(4)]
            got = jnp.concatenate(got, axis=1)
            gq_o[rows, lo:hi] = got[:, :HALF]
            gk_o[rows, lo:hi] = got[:, HALF : 2 * HALF]
            gv_o[rows, lo:hi] = got[:, 2 * HALF :]


def shape(dims, kind):
    return jax.ShapeDtypeStruct(dims, kind)


def shards(
    frame_in,
    token_ids,
    durations,
    valid_len,
    t_bin,
    token_table,
    enc_weight,
    mod_table,
    w_query,
    w_key,
    w_value,
    attn_grad,
):
    vm = pl.BlockSpec(memory_space=pltpu.VMEM)
    sm = pl.BlockSpec(memory_space=pltpu.SMEM)
    hb = pl.BlockSpec(memory_space=pl.ANY)
    att, fg, fin = pl.pallas_call(
        window_kernel,
        name="window",
        out_shape=(
            shape((2, NF, HALF), BF16),
            shape((NF, D), BF16),
            shape((2, NY, 16, SC), BF16),
        ),
        in_specs=[sm] * 2 + [vm] * 6 + [hb] * 4,
        out_specs=(vm,) * 3,
        scratch_shapes=[
            pltpu.VMEM((NF, D), BF16),
            pltpu.VMEM((NF, QW), BF16),
            pltpu.VMEM((QW, D), BF16),
            pltpu.VMEM((64, 2 * D), F32),
            pltpu.VMEM((NX, NZ, PIECE, 128), BF16),
            pltpu.VMEM((NX, NZ, 32, HALF), BF16),
            pltpu.VMEM((2, NX, NZ, 32, 128), BF16),
            pltpu.VMEM((2, NX, NZ, 32, 128), BF16),
            pltpu.VMEM((GROUP, 8, 128), F32),
            pltpu.VMEM((GROUP, 64, 128), BF16),
            pltpu.VMEM((GROUP, 64, 128), BF16),
            pltpu.VMEM((2, NF, D), BF16),
            pltpu.VMEM((NF, D), F32),
            pltpu.VMEM((NF, HALF), BF16),
            pltpu.VMEM((2, NF, HALF), BF16),
            pltpu.VMEM((2, NF, HALF), BF16),
            pltpu.VMEM((2, 2, 6 * BLK, HALF), BF16),
            pltpu.VMEM((2, NF, HALF), BF16),
            pltpu.VMEM((2, 6 * BLK, 2 * HALF), F32),
            pltpu.VMEM((2, 2 * BLK, 2 * HALF), BF16),
            pltpu.VMEM((2, BLK, 2 * HALF), BF16),
            pltpu.VMEM((2, 2 * BLK, 2 * HALF), BF16),
            pltpu.VMEM((2, BLK, 2 * HALF), BF16),
            pltpu.VMEM((NF, HALF), BF16),
            pltpu.VMEM((NF, D), BF16),
            pltpu.VMEM((NF, D), BF16),
            pltpu.VMEM((NX, NZ, 32, AC), BF16),
            pltpu.VMEM((NX, NZ, 32, HALF), BF16),
            pltpu.VMEM((4, NX, 32, AC), BF16),
            pltpu.VMEM((3, NX, 32, AC), BF16),
            pltpu.VMEM((NX, 32, AC), BF16),
            pltpu.VMEM((3, 32, AC), BF16),
            pltpu.VMEM((3, NZ, 32, HALF), BF16),
            pltpu.VMEM((NZ, 32, HALF), BF16),
            pltpu.VMEM((7, 32, HALF), BF16),
            pltpu.VMEM((NY, 16, SC), BF16),
            pltpu.VMEM((NY - 1, 16, SC), BF16),
            pltpu.SemaphoreType.DMA((4,)),
            pltpu.SemaphoreType.DMA((220,)),
            pltpu.SemaphoreType.DMA((220,)),
        ],
        compiler_params=pltpu.CompilerParams(
            collective_id=0, has_side_effects=True, vmem_limit_bytes=VMEM_LIMIT
        ),
    )(
        t_bin,
        valid_len,
        token_ids[0],
        durations[0],
        token_table,
        w_query,
        w_key,
        w_value,
        frame_in[0],
        attn_grad[0],
        enc_weight,
        mod_table,
    )
    att, fg, gq, gk, gv = pl.pallas_call(
        finish_kernel,
        name="finish",
        out_shape=(
            shape((NF, QW), BF16),
            shape((NF, D), BF16),
            shape((32, QW), F32),
            shape((32, QW), F32),
            shape((32, QW), F32),
        ),
        in_specs=[vm] * 3,
        out_specs=(vm,) * 5,
    )(att, fg, fin)
    return att[None], fg[None], gq, gk, gv


def solution(mesh):
    placed = (
        P("dp", "seq", None),
        P("dp", "seq", None),
        P("dp", "seq", None),
        P("dp"),
        P("dp"),
        P("seq", None),
        P(),
        P(),
        P("seq", None),
        P("seq", None),
        P("seq", None),
        P("dp", "seq", None),
    )
    return jax.shard_map(
        shards,
        mesh=mesh,
        in_specs=placed,
        out_specs=(
            P("dp", "seq", None),
            P("dp", "seq", None),
            P("seq", None),
            P("seq", None),
            P("seq", None),
        ),
        check_vma=False,
    )
```

```python
import math

import jax
import jax.numpy as jnp
from jax import lax
from jax.experimental import pallas as pl
from jax.experimental.pallas import tpu as pltpu
from jax.sharding import PartitionSpec as P

D = 1024
QW = 512
BLK = 48
NF = 144
NX = 4
NY = 8
NZ = 8
N_SEQ = NX * NZ
PIECE = 64
HALF = 256
WC = 3 * HALF
AC = 2 * HALF
SC = WC // 4
GROUP = 8
MESH = pl.DeviceIdType.MESH
F32 = jnp.float32
BF16 = jnp.bfloat16
VMEM_LIMIT = 56 * 1024 * 1024


class Place:
    def __init__(self):
        self.dp = lax.axis_index("dp")
        self.seq = lax.axis_index("seq")
        self.c = lax.rem(self.dp, 2)
        self.y = self.dp // 2
        self.x = self.seq // NZ
        self.z = lax.rem(self.seq, NZ)
        self.sign = 1 - 2 * self.c
        self.q = lax.rem(self.dp, GROUP)

    def xs(self, o):
        return lax.rem(self.x + o * self.sign + NX, NX)

    def zs(self, o):
        return lax.rem(self.z + o * self.sign + NZ, NZ)

    def x_dev(self, o):
        return (self.dp, self.xs(o) * NZ + self.z)

    def z_dev(self, o):
        return (self.dp, self.x * NZ + self.zs(o))

    def seq_dev(self, o):
        return (self.dp, lax.rem(self.seq + o + N_SEQ, N_SEQ))

    def sib(self):
        return (self.dp + self.sign, self.seq)

    def mate(self, d):
        return lax.rem(self.q + d, GROUP)

    def mate_dev(self, d):
        return (self.dp - self.q + self.mate(d), self.seq)

    def y_dev(self, d):
        return (lax.rem(self.y + d, NY) * 2 + self.c, self.seq)


def nn(a, b):
    return jnp.dot(a, b, preferred_element_type=F32)


def nt(a, b):
    return lax.dot_general(a, b, (((1,), (1,)), ((), ())), preferred_element_type=F32)


def tn(a, b):
    return lax.dot_general(a, b, (((0,), (0,)), ((), ())), preferred_element_type=F32)


def add(a, b):
    return a.astype(F32) + b.astype(F32)


def pick(index, parts):
    out = parts[0]
    for i in range(1, len(parts)):
        out = jnp.where(index == i, parts[i], out)
    return out


X_OFFS = (1, -1, 2)
Z_OFFS = (1, -1, 2, -2, 3, -3, 4)


def window_kernel(
    t_bin,
    valid,
    ids,
    dur,
    table,
    wq,
    wk,
    wv,
    frame_h,
    grad_h,
    enc_h,
    mod_h,
    att_o,
    fg_o,
    fin,
    frame,
    grad,
    enc,
    mod,
    tbuf,
    wbuf,
    wmine,
    wswap,
    idb,
    esend,
    embb,
    modb,
    nrm,
    gsend,
    gradb,
    qb,
    kvb,
    dqb,
    ext,
    hps,
    hns,
    hpr,
    hnr,
    osend,
    hsend,
    hrecv,
    pa,
    pb,
    azr,
    azl,
    qa,
    axr,
    bxr,
    qvb,
    bzr,
    part,
    yb,
    lsem,
    ssem,
    rsem,
):
    me = Place()
    c = me.c
    loads = []
    for i, (a, b) in enumerate(
        ((grad_h, grad), (frame_h, frame), (enc_h, enc), (mod_h, mod))
    ):
        loads.append(pltpu.make_async_copy(a, b, lsem.at[i]))
        loads[i].start()
    quarter = pick(
        lax.rem(me.q, 4), [table[:, i * 128 : (i + 1) * 128].astype(F32) for i in range(4)]
    )
    upper = me.q // 4
    odd = lax.rem(me.y, 2)
    tbuf[me.x, me.z] = pick(
        upper,
        [
            quarter[:PIECE],
            jnp.concatenate(
                [quarter[PIECE:], jnp.zeros((2 * PIECE - 104, 128), F32)], axis=0
            ),
        ],
    ).astype(BF16)
    w_q, w_k, w_v = [pick(c, [r[:, :HALF], r[:, HALF:]]) for r in (wq, wk, wv)]
    wbuf[me.x, me.z] = w_k
    w_m = pick(odd, [w_q, w_v])
    for i in range(2):
        wmine[i, me.x, me.z] = w_m[:, i * 128 : (i + 1) * 128]
    idb[me.q] = jnp.where(
        lax.broadcasted_iota(jnp.int32, (8, 128), 0) == 0,
        jnp.concatenate([ids[...].astype(F32), jnp.zeros((1, 68), F32)], axis=1),
        valid[0].astype(F32),
    )
    barrier = pltpu.get_barrier_semaphore()
    peers = [me.y_dev(d) for d in range(1, NY)]
    peers += [me.mate_dev(d) for d in range(1, GROUP, 2)]
    peers += [me.x_dev(o) for o in X_OFFS] + [me.z_dev(o) for o in Z_OFFS]
    peers += [me.seq_dev(1), me.seq_dev(-1)]
    for dev in peers:
        pl.semaphore_signal(barrier, inc=1, device_id=dev, device_id_type=MESH)
    pl.semaphore_wait(barrier, len(peers))
    started = []

    def rc(src, dst, dev):
        i = len(started)
        cp = pltpu.make_async_remote_copy(
            src_ref=src,
            dst_ref=dst,
            send_sem=ssem.at[i],
            recv_sem=rsem.at[i],
            device_id=dev,
            device_id_type=MESH,
        )
        cp.start()
        started.append(cp)
        return cp

    def same(ref, dev):
        return rc(ref, ref, dev)

    def cut(src, dst, dev, size):
        rows = [pl.ds(i, size) for i in range(0, src.shape[0], size)]
        return [rc(src.at[r], dst.at[r], dev) for r in rows]

    drained = [0]

    def drain():
        for cp in started[drained[0] :]:
            cp.wait_send()
        drained[0] = len(started)

    def arrive(cps):
        for cp in cps:
            cp.wait_recv()

    def t_at(xo, zo):
        return tbuf.at[me.xs(xo), me.zs(zo)]

    def w_at(xo, zo):
        return wbuf.at[me.xs(xo), me.zs(zo)]

    id_cp = [same(idb.at[me.q], me.mate_dev(d)) for d in range(1, GROUP)]
    t_z = {o: same(t_at(0, 0), me.z_dev(o)) for o in Z_OFFS}
    t_x = {}

    def t_x_send(zo):
        for xo in X_OFFS:
            t_x[xo, zo] = same(t_at(0, zo), me.x_dev(xo))

    w_r, w_l = {}, {}

    def w_start(xo):
        w_r[xo, 1] = same(w_at(xo, 0), me.z_dev(1))
        w_l[xo, 1] = same(w_at(xo, 0), me.z_dev(-1))

    def w_step(xo, k):
        w_r[xo, k].wait_recv()
        if k < 4:
            w_r[xo, k + 1] = same(w_at(xo, -k), me.z_dev(1))
            w_l[xo, k].wait_recv()
        if k < 3:
            w_l[xo, k + 1] = same(w_at(xo, k), me.z_dev(-1))

    w_y = []

    def y_send(xo):
        for i, d in ((0, 1), (1, NY - 1)):
            w_y.append(
                rc(wmine.at[i, me.xs(xo)], wswap.at[i, me.xs(xo)], me.y_dev(d))
            )

    W_ROWS = (0, -1, 1, 2)

    def w_steps(k):
        for xo in W_ROWS:
            w_step(xo, k)

    w_x = {o: same(w_at(0, 0), me.x_dev(o)) for o in X_OFFS}
    t_x_send(0)
    w_start(0)
    wm_z = [same(wmine.at[:, me.x, me.z], me.z_dev(o)) for o in Z_OFFS]
    loads[0].wait()
    gsend[...] = pick(c, [grad[:, HALF:], grad[:, :HALF]])
    gradb[0] = pick(c, [grad[:, :HALF], grad[:, HALF:]])
    g_cp = cut(gsend, gradb.at[1], me.sib(), 48)

    lane = lax.broadcasted_iota(jnp.int32, (64, 60), 1)
    row = lax.broadcasted_iota(jnp.int32, (64, 60), 0)
    end_col = jnp.sum(
        jnp.where(lane <= row, dur[...].astype(F32), 0.0), axis=1, keepdims=True
    )
    frame_pos = lax.broadcasted_iota(jnp.int32, (64, NF), 1).astype(F32)
    tok_pos = lax.broadcasted_iota(jnp.int32, (64, NF), 0).astype(F32)
    owner = jnp.sum(jnp.where(end_col <= frame_pos, 1.0, 0.0), axis=0, keepdims=True)
    spread = jnp.where(tok_pos == owner, 1.0, 0.0).astype(BF16)
    for cp in id_cp:
        cp.wait_recv()
    lane = lax.broadcasted_iota(jnp.int32, (64, 128), 1)
    row = lax.broadcasted_iota(jnp.int32, (64, 128), 0)
    id_cols = []
    for i in range(GROUP):
        row_ids = idb[i][:1]
        owner_row = jnp.floor((row_ids + 0.5) * (1.0 / 104.0))
        inner = row_ids - 104.0 * owner_row - (PIECE * upper).astype(F32)
        held = (inner >= 0.0) & (inner < float(PIECE))
        row_ids = jnp.where(held, owner_row * PIECE + inner, -1.0)
        id_cols.append(
            jnp.sum(jnp.where(lane == row, row_ids, 0.0), axis=1, keepdims=True)
        )
    id_col = jnp.concatenate(id_cols, axis=0)
    vocab_pos = lax.broadcasted_iota(jnp.int32, (GROUP * 64, NZ * PIECE), 1)
    vocab_pos = vocab_pos.astype(F32)

    def emb_part(xo):
        base = (me.xs(xo) * (NZ * PIECE)).astype(F32)
        hot = jnp.where(id_col - base == vocab_pos, 1.0, 0.0).astype(BF16)
        return nn(hot, tbuf[me.xs(xo)].reshape(NZ * PIECE, 128))

    for o in (1, -1):
        t_z[o].wait_recv()
        t_x_send(-o)
    for o in (1, -1, 2):
        w_x[o].wait_recv()
        w_start(-o if o != 2 else 2)
    for o in (2, -2, 3, -3, 4):
        t_z[o].wait_recv()
        t_x_send(-o if o != 4 else 4)
    w_steps(1)
    arrive(wm_z)
    wm_x = {o: same(wmine.at[:, me.x], me.x_dev(o)) for o in X_OFFS}
    y_send(0)
    emb = emb_part(0)
    for zo in (0,) + Z_OFFS:
        t_x[1, zo].wait_recv()
    w_steps(2)
    emb += emb_part(-1)
    for o, xo in ((-1, 1), (2, 2)):
        for zo in (0,) + Z_OFFS:
            t_x[o, zo].wait_recv()
        emb += emb_part(xo)
    esend[...] = emb.astype(BF16).reshape(GROUP, 64, 128)
    embb[me.q] = esend[me.q]
    e_cp = [
        rc(esend.at[me.mate(d)], embb.at[me.q], me.mate_dev(d)) for d in range(1, GROUP)
    ]
    w_steps(3)
    for o in X_OFFS:
        wm_x[o].wait_recv()
        y_send(-o if o != 2 else 2)
    arrive(e_cp)
    tok_emb = jnp.concatenate(
        [add(embb[i], embb[i + 4]).astype(BF16) for i in range(4)], axis=1
    )
    frame_emb = tn(spread, tok_emb).astype(BF16)
    for cp in loads[1:]:
        cp.wait()
    hidden = frame[...].astype(F32) + nn(frame_emb, enc[...])
    root = jnp.sqrt(jnp.mean(hidden * hidden, axis=1, keepdims=True) + 1e-06)
    normed = hidden / root
    picked = mod[pl.ds(t_bin[0], 1), :]
    gain = 1.0 + picked[:, :D]
    nrm[...] = normed
    modb[0] = (normed * gain + picked[:, D:]).astype(BF16)
    m_cp = cut(modb.at[0], modb.at[1], me.sib(), 16)
    w_steps(4)

    halos = {}

    def send_halo(r, i):
        halos[r] = halos.get(r, []) + [
            rc(
                kvb.at[i, r, 3 * BLK : 5 * BLK],
                kvb.at[i, r, : 2 * BLK],
                me.seq_dev(1),
            ),
            rc(
                kvb.at[i, r, 2 * BLK : 3 * BLK],
                kvb.at[i, r, 5 * BLK :],
                me.seq_dev(-1),
            ),
        ]

    w_key = wbuf[...].reshape(D, HALF)
    for r in range(2):
        if r == 1:
            arrive(m_cp)
        kvb[0, r, 2 * BLK : 5 * BLK] = nn(modb[r], w_key).astype(BF16)
        send_halo(r, 0)
    w_mine = jnp.concatenate([wmine[i].reshape(D, 128) for i in range(2)], axis=1)
    mine_r = [nn(modb[r], w_mine) for r in range(2)]
    arrive(w_y)
    w_swap = jnp.concatenate([wswap[i].reshape(D, 128) for i in range(2)], axis=1)
    for r in range(2):
        swap_r = nn(modb[r], w_swap)
        kvb[1, r, 2 * BLK : 5 * BLK] = pick(odd, [swap_r, mine_r[r]]).astype(BF16)
        send_halo(r, 1)
        qb[r] = pick(odd, [mine_r[r], swap_r]).astype(BF16)
    drain()
    arrive(g_cp)

    start = me.seq * NF
    head = lax.broadcasted_iota(jnp.int32, (BLK, HALF), 1) // 64
    q_off = lax.broadcasted_iota(jnp.int32, (BLK, 4 * BLK), 0)
    k_off = lax.broadcasted_iota(jnp.int32, (BLK, 4 * BLK), 1)
    live_row = lax.broadcasted_iota(jnp.int32, (BLK, HALF), 0)
    ext[...] = jnp.zeros_like(ext)

    def stacked(block):
        return jnp.concatenate(
            [jnp.where(head == i, block, 0.0) for i in range(4)], axis=0
        ).astype(BF16)

    def merged(rows):
        return pick(head, [rows[i * BLK : (i + 1) * BLK] for i in range(4)]).astype(BF16)

    back = {}
    for r in range(2):
        for cp in halos[r]:
            cp.wait_recv()
        slot = me.q if r == 0 else me.q + me.sign
        valid_end = idb[slot][1:2, 0:1]
        for b in range(3):
            q_pos = start + b * BLK + q_off
            k_pos = start + (b - 2) * BLK + k_off
            inside = (k_pos >= 0) & (k_pos < N_SEQ * NF)
            open_pair = (k_pos.astype(F32) < valid_end) | (q_pos.astype(F32) >= valid_end)
            bias = jnp.where(inside & open_pair, 0.0, -1e30)
            bias = jnp.concatenate([bias] * 4, axis=0)
            live = (start + b * BLK + live_row).astype(F32) < valid_end
            mine = slice(b * BLK, (b + 1) * BLK)
            window = slice(b * BLK, (b + 4) * BLK)
            q_rows = stacked(qb[r, mine].astype(F32))
            g_rows = stacked(jnp.where(live, gradb[r, mine].astype(F32), 0.0))
            keys = kvb[0, r, window]
            values = kvb[1, r, window]
            scores = nt(q_rows, keys) * 0.125 + bias
            top = jnp.max(scores, axis=1, keepdims=True)
            e = jnp.where(bias < 0.0, 0.0, jnp.exp(scores - top))
            prob = e / jnp.sum(e, axis=1, keepdims=True)
            low = prob.astype(BF16)
            mixed = merged(nn(low, values))
            if r == 0:
                att_o[c, mine] = mixed
            else:
                osend[mine] = mixed
            g_prob = nt(g_rows, values)
            centre = jnp.sum(prob * g_prob, axis=1, keepdims=True)
            g_score = (prob * (g_prob - centre) * 0.125).astype(BF16)
            dqb[r, mine] = merged(nn(g_score, keys))
            ext[r, window, :HALF] += tn(g_score, q_rows)
            ext[r, window, HALF:] += tn(low, g_rows)
            if b == 1:
                hps[r] = ext[r, : 2 * BLK].astype(BF16)
                back[r] = cut(hps.at[r], hpr.at[r], me.seq_dev(-1), BLK)
        hns[r] = ext[r, 5 * BLK :].astype(BF16)
        back[r].append(rc(hns.at[r], hnr.at[r], me.seq_dev(1)))
    o_cp = cut(osend, att_o.at[c], me.sib(), BLK)
    scale = 1.0 / math.sqrt(16 * 4608)
    b_x, a_r, a_l = {}, {}, {}
    A_ROWS = (2, 1, -1, 0)

    def term_of(xi, pair):
        cols = pl.ds(pl.multiple_of(xi * HALF, HALF), HALF)
        term = tn(modb[0, :, cols], pair[0]) + tn(modb[1, :, cols], pair[1])
        return (term * scale).astype(BF16)

    def a_start(i, xo, term):
        xi = me.xs(xo)
        pa[i, xi] = term.reshape(NZ, 32, HALF)
        a_r[i, xo, 1] = rc(pa.at[i, xi, me.zs(4)], azr.at[i, 0, xi], me.z_dev(1))
        a_l[i, xo, 1] = rc(pa.at[i, xi, me.zs(-3)], azl.at[i, 0, xi], me.z_dev(-1))

    def a_step(i, k):
        for xo in A_ROWS:
            xi = me.xs(xo)
            a_r[i, xo, k].wait_recv()
            if k < 4:
                azr[i, k - 1, xi] = add(azr[i, k - 1, xi], pa[i, xi, me.zs(4 - k)]).astype(BF16)
                a_r[i, xo, k + 1] = rc(azr.at[i, k - 1, xi], azr.at[i, k, xi], me.z_dev(1))
                a_l[i, xo, k].wait_recv()
            if k < 3:
                azl[i, k - 1, xi] = add(azl[i, k - 1, xi], pa[i, xi, me.zs(k - 3)]).astype(BF16)
                a_l[i, xo, k + 1] = rc(azl.at[i, k - 1, xi], azl.at[i, k, xi], me.z_dev(-1))

    for xo in A_ROWS:
        a_start(0, xo, term_of(me.xs(xo), [dqb[0], dqb[1]]))
    dkv = []
    for r in range(2):
        arrive(back[r])
        own = ext[r, 2 * BLK : 5 * BLK]
        dkv.append(
            jnp.concatenate(
                [own[:BLK] + hnr[r].astype(F32), own[BLK:] + hpr[r].astype(F32)], axis=0
            ).astype(BF16)
        )
    for xo in A_ROWS:
        xi = me.xs(xo)
        term = term_of(xi, dkv)
        a_start(1, xo, term[:, :HALF])
        pb[xi] = term[:, HALF:].reshape(NZ, 32, HALF)
        if xo != 0:
            b_x[xo] = rc(pb.at[xi], bxr.at[X_OFFS.index(xo)], me.x_dev(xo))
    a_step(0, 1)
    grads = [jnp.concatenate([dqb[r], dkv[r]], axis=1) for r in range(2)]

    def hidden_part(g):
        g_q, g_k, g_v = g[:, :HALF], g[:, HALF : 2 * HALF], g[:, 2 * HALF :]
        return (
            nt(g_k, w_key)
            + nt(pick(odd, [g_q, g_v]), w_mine)
            + nt(pick(odd, [g_v, g_q]), w_swap)
        )

    hsend[...] = hidden_part(grads[1]).astype(BF16)
    h_cp = cut(hsend, hrecv, me.sib(), 16)
    a_step(1, 1)
    a_step(0, 2)
    hidden_grad = hidden_part(grads[0])
    a_step(1, 2)
    for cp in b_x.values():
        cp.wait_recv()
    total = pb[me.x].astype(F32)
    for i in range(3):
        total = total + bxr[i].astype(F32)
    qvb[...] = total.astype(BF16)
    b_z = [
        rc(qvb.at[me.zs(o)], bzr.at[i], me.z_dev(o)) for i, o in enumerate(Z_OFFS)
    ]
    a_step(0, 3)
    a_step(1, 3)
    arrive(h_cp)
    scaled = (hidden_grad + hrecv[...].astype(F32)) * gain
    normed = nrm[...]
    fg_o[...] = (
        (scaled - normed * jnp.mean(scaled * normed, axis=1, keepdims=True)) / root
    ).astype(BF16)
    for i in range(2):
        a_step(i, 4)
        for xo in A_ROWS:
            xi = me.xs(xo)
            got = add(azr[i, 3, xi], azl[i, 2, xi]) + pa[i, xi, me.z].astype(F32)
            qa[xi, :, i * HALF : (i + 1) * HALF] = got.astype(BF16)
    a_x = [rc(qa.at[me.xs(o)], axr.at[i], me.x_dev(o)) for i, o in enumerate(X_OFFS)]
    sum_b = qvb[me.z].astype(F32)
    for i, cp in enumerate(b_z):
        cp.wait_recv()
        sum_b = sum_b + bzr[i].astype(F32)
    sum_a = qa[me.x].astype(F32)
    for i, cp in enumerate(a_x):
        cp.wait_recv()
        sum_a = sum_a + axr[i].astype(F32)
    whole = jnp.concatenate([sum_a, sum_b], axis=1)
    for i in range(NY):
        rows, cols = slice(i // 4 * 16, i // 4 * 16 + 16), slice(i % 4 * SC, (i % 4 + 1) * SC)
        part[i] = whole[rows, cols].astype(BF16)

    y_cp = [
        rc(part.at[lax.rem(me.y + d, NY)], yb.at[d - 1], me.y_dev(d))
        for d in range(1, NY)
    ]
    drain()
    total = part[me.y].astype(F32)
    for d in range(1, NY):
        y_cp[d - 1].wait_recv()
        total = total + yb[d - 1].astype(F32)
    fin[c, me.y] = total.astype(BF16)
    eighth = fin.at[c, me.y]
    y_all = [same(eighth, me.y_dev(d)) for d in range(1, NY)]
    last = [same(eighth, me.sib())]
    for d in range(1, NY):
        y_all[d - 1].wait_recv()
        last.append(same(fin.at[c, lax.rem(me.y - d + NY, NY)], me.sib()))
    arrive(last)
    arrive(o_cp)
    drain()


def finish_kernel(att, fg, fin, att_o, fg_o, gq_o, gk_o, gv_o):
    fg_o[...] = fg[...]
    for h in range(2):
        lo, hi = h * HALF, (h + 1) * HALF
        att_o[:, lo:hi] = att[h]
        for rt in range(2):
            rows = slice(16 * rt, 16 * rt + 16)
            got = [fin[h, 4 * rt + j].astype(F32) for j in range(4)]
            got = jnp.concatenate(got, axis=1)
            gq_o[rows, lo:hi] = got[:, :HALF]
            gk_o[rows, lo:hi] = got[:, HALF : 2 * HALF]
            gv_o[rows, lo:hi] = got[:, 2 * HALF :]


def shape(dims, kind):
    return jax.ShapeDtypeStruct(dims, kind)


def shards(
    frame_in,
    token_ids,
    durations,
    valid_len,
    t_bin,
    token_table,
    enc_weight,
    mod_table,
    w_query,
    w_key,
    w_value,
    attn_grad,
):
    vm = pl.BlockSpec(memory_space=pltpu.VMEM)
    sm = pl.BlockSpec(memory_space=pltpu.SMEM)
    hb = pl.BlockSpec(memory_space=pl.ANY)
    att, fg, fin = pl.pallas_call(
        window_kernel,
        name="window",
        out_shape=(
            shape((2, NF, HALF), BF16),
            shape((NF, D), BF16),
            shape((2, NY, 16, SC), BF16),
        ),
        in_specs=[sm] * 2 + [vm] * 6 + [hb] * 4,
        out_specs=(vm,) * 3,
        scratch_shapes=[
            pltpu.VMEM((NF, D), BF16),
            pltpu.VMEM((NF, QW), BF16),
            pltpu.VMEM((QW, D), BF16),
            pltpu.VMEM((64, 2 * D), F32),
            pltpu.VMEM((NX, NZ, PIECE, 128), BF16),
            pltpu.VMEM((NX, NZ, 32, HALF), BF16),
            pltpu.VMEM((2, NX, NZ, 32, 128), BF16),
            pltpu.VMEM((2, NX, NZ, 32, 128), BF16),
            pltpu.VMEM((GROUP, 8, 128), F32),
            pltpu.VMEM((GROUP, 64, 128), BF16),
            pltpu.VMEM((GROUP, 64, 128), BF16),
            pltpu.VMEM((2, NF, D), BF16),
            pltpu.VMEM((NF, D), F32),
            pltpu.VMEM((NF, HALF), BF16),
            pltpu.VMEM((2, NF, HALF), BF16),
            pltpu.VMEM((2, NF, HALF), BF16),
            pltpu.VMEM((2, 2, 6 * BLK, HALF), BF16),
            pltpu.VMEM((2, NF, HALF), BF16),
            pltpu.VMEM((2, 6 * BLK, 2 * HALF), F32),
            pltpu.VMEM((2, 2 * BLK, 2 * HALF), BF16),
            pltpu.VMEM((2, BLK, 2 * HALF), BF16),
            pltpu.VMEM((2, 2 * BLK, 2 * HALF), BF16),
            pltpu.VMEM((2, BLK, 2 * HALF), BF16),
            pltpu.VMEM((NF, HALF), BF16),
            pltpu.VMEM((NF, D), BF16),
            pltpu.VMEM((NF, D), BF16),
            pltpu.VMEM((2, NX, NZ, 32, HALF), BF16),
            pltpu.VMEM((NX, NZ, 32, HALF), BF16),
            pltpu.VMEM((2, 4, NX, 32, HALF), BF16),
            pltpu.VMEM((2, 3, NX, 32, HALF), BF16),
            pltpu.VMEM((NX, 32, AC), BF16),
            pltpu.VMEM((3, 32, AC), BF16),
            pltpu.VMEM((3, NZ, 32, HALF), BF16),
            pltpu.VMEM((NZ, 32, HALF), BF16),
            pltpu.VMEM((7, 32, HALF), BF16),
            pltpu.VMEM((NY, 16, SC), BF16),
            pltpu.VMEM((NY - 1, 16, SC), BF16),
            pltpu.SemaphoreType.DMA((4,)),
            pltpu.SemaphoreType.DMA((250,)),
            pltpu.SemaphoreType.DMA((250,)),
        ],
        compiler_params=pltpu.CompilerParams(
            collective_id=0, has_side_effects=True, vmem_limit_bytes=VMEM_LIMIT
        ),
    )(
        t_bin,
        valid_len,
        token_ids[0],
        durations[0],
        token_table,
        w_query,
        w_key,
        w_value,
        frame_in[0],
        attn_grad[0],
        enc_weight,
        mod_table,
    )
    att, fg, gq, gk, gv = pl.pallas_call(
        finish_kernel,
        name="finish",
        out_shape=(
            shape((NF, QW), BF16),
            shape((NF, D), BF16),
            shape((32, QW), F32),
            shape((32, QW), F32),
            shape((32, QW), F32),
        ),
        in_specs=[vm] * 3,
        out_specs=(vm,) * 5,
    )(att, fg, fin)
    return att[None], fg[None], gq, gk, gv


def solution(mesh):
    placed = (
        P("dp", "seq", None),
        P("dp", "seq", None),
        P("dp", "seq", None),
        P("dp"),
        P("dp"),
        P("seq", None),
        P(),
        P(),
        P("seq", None),
        P("seq", None),
        P("seq", None),
        P("dp", "seq", None),
    )
    return jax.shard_map(
        shards,
        mesh=mesh,
        in_specs=placed,
        out_specs=(
            P("dp", "seq", None),
            P("dp", "seq", None),
            P("seq", None),
            P("seq", None),
            P("seq", None),
        ),
        check_vma=False,
    )
```
